256 devices in a mesh: row: 16 (over x, y_hi, core), col: 16 (over y_lo, z).
Axes of the slice: x: 4, y: 4 (y_hi: 2, y_lo: 2; y = y_hi * 2 + y_lo), z: 8, core: 2. Of those that a mesh axis runs over, the one named last changes fastest.
Arguments:
- latents: bfloat16 [2048, 6144], P('col', 'row'), may hold values from -6 to 6
- w_in: bfloat16 [6144, 24576], P('row', 'col'), may hold values from -0.078125 to 0.078125
- w_out: bfloat16 [24576, 6144], P('col', 'row'), may hold values from -0.0390625 to 0.0390625
- cotangent: bfloat16 [2048, 6144], P('col', 'row'), may hold values from -0.3125 to 0.3125
Outputs:
- mixed: bfloat16 [2048, 6144], P('col', 'row')
- grad_w_in: bfloat16 [6144, 24576], P('row', 'col')
- grad_w_out: bfloat16 [24576, 6144], P('col', 'row')
The draws below stay inside these ranges and needn't reach their ends.
All inputs are finite; a program needn't handle non-finite values.
Results may differ from the reference program's by a relative error of at most 0.03.
Values may be sent and summed in bfloat16 or wider, within the bound.
A program may use at most 128 MiB of HBM per device.

```python
import jax
import jax.numpy as jnp
from jax import lax

D = 6144
H = 24576
TOKENS = 2048
N_ROW = 16
N_COL = 16


def steps_of(stream_key, dims, shards, least, high):
    level, own = 1.0, jax.random.fold_in(stream_key, 6)
    for position, blocks in shards:
        heights = jnp.exp(jax.random.uniform(jax.random.fold_in(own, position), (blocks,), jnp.float32, least / len(shards), high / len(shards)))
        level = level * jnp.repeat(heights, dims[position] // blocks).reshape([-1 if axis == position else 1 for axis in range(len(dims))])
    return level


def gaussian(rng, extent, width, reach, shards=(), dtype=jnp.bfloat16):
    level = steps_of(rng, extent, shards, -0.22, 0.18) if shards else 1.0
    drawn = jax.random.normal(rng, extent, jnp.float32) * width * level
    return jnp.minimum(jnp.maximum(drawn, -reach), reach).astype(dtype)


def setup_inputs(seed: int = 0) -> dict:
    keys = jax.random.split(jax.random.key(seed), 5)
    latents = gaussian(keys[0], (TOKENS, D), 1.0, 6.0, ((0, 16), (1, 16)))
    w_in = gaussian(keys[1], (D, H), D ** -0.5, 0.078125, ((0, 16), (1, 16)))
    w_out = gaussian(keys[2], (H, D), H ** -0.5, 0.0390625, ((0, 16), (1, 16)))
    cotangent = gaussian(keys[3], (TOKENS, D), (TOKENS ** -0.5), 0.3125, ((0, 16), (1, 16)))
    return dict(latents=latents, w_in=w_in, w_out=w_out, cotangent=cotangent)


def gelu_parts(hidden):
    cdf = 0.5 * (1.0 + jax.scipy.special.erf(hidden * 0.7071067811865476))
    pdf = jnp.exp(-0.5 * hidden * hidden) * 0.3989422804014327
    return hidden * cdf, cdf + hidden * pdf


def reference(latents, w_in, w_out, cotangent):
    width_block = D // N_ROW
    hidden_block = H // N_COL

    def hidden_step(index, total):
        start = (index * width_block).astype(jnp.int32)
        feature_part = lax.dynamic_slice_in_dim(latents, start, width_block, 1)
        weight_part = lax.dynamic_slice_in_dim(w_in, start, width_block, 0)
        term = jnp.dot(feature_part, weight_part, preferred_element_type=jnp.float32)
        rounded = lax.optimization_barrier(term.astype(jnp.bfloat16))
        return total + rounded.astype(jnp.float32)

    hidden = lax.fori_loop(0, N_ROW, hidden_step, jnp.zeros((TOKENS, H), jnp.float32))
    act, slope = gelu_parts(hidden)
    act = act.astype(jnp.bfloat16)

    def mixed_step(index, total):
        start = (index * hidden_block).astype(jnp.int32)
        act_part = lax.dynamic_slice_in_dim(act, start, hidden_block, 1)
        weight_part = lax.dynamic_slice_in_dim(w_out, start, hidden_block, 0)
        term = jnp.dot(act_part, weight_part, preferred_element_type=jnp.float32)
        rounded = lax.optimization_barrier(term.astype(jnp.bfloat16))
        return total + rounded.astype(jnp.float32)

    mixed = lax.fori_loop(0, N_COL, mixed_step, jnp.zeros((TOKENS, D), jnp.float32)).astype(jnp.bfloat16)

    def act_step(index, total):
        start = (index * width_block).astype(jnp.int32)
        grad_part = lax.dynamic_slice_in_dim(cotangent, start, width_block, 1)
        weight_part = lax.dynamic_slice_in_dim(w_out, start, width_block, 1)
        term = lax.dot_general(grad_part, weight_part, (((1,), (1,)), ((), ())), preferred_element_type=jnp.float32)
        rounded = lax.optimization_barrier(term.astype(jnp.bfloat16))
        return total + rounded.astype(jnp.float32)

    grad_act = lax.fori_loop(0, N_ROW, act_step, jnp.zeros((TOKENS, H), jnp.float32))
    grad_hidden = (grad_act * slope).astype(jnp.bfloat16)
    grad_w_out = lax.dot_general(act, cotangent, (((0,), (0,)), ((), ())), preferred_element_type=jnp.float32).astype(jnp.bfloat16)
    grad_w_in = lax.dot_general(latents, grad_hidden, (((0,), (0,)), ((), ())), preferred_element_type=jnp.float32).astype(jnp.bfloat16)
    return mixed, grad_w_in, grad_w_out
```

```python
import jax
import jax.numpy as jnp
from jax import lax
from jax.experimental import pallas as pl
from jax.experimental.pallas import tpu as pltpu
from jax.sharding import PartitionSpec as P

MESH = pl.DeviceIdType.MESH
BF = jnp.bfloat16
F32 = jnp.float32

TOK, FEAT, HID = 128, 384, 1536
ROWS, WIDE = 256, 768
CH = 8
PIECE, HALF = 64, 32

NN = (((1,), (0,)), ((), ()))
NT = (((1,), (1,)), ((), ()))
TN = (((0,), (0,)), ((), ()))


def dot(a, b, dims):
    return lax.dot_general(a, b, dims, preferred_element_type=F32)


def kernel(
    lat, w_in, w_out, cot,
    mixed, g_in, g_out,
    X, WI, WO, PT, FAR, CMB, RX, YS, YR, HS, SL, A, MO, MS, MR, MT, MIX, OUT, GW, GB,
    s_loc, s_w, s_ws, s_x, s_xs, s_c, s_cs, s_far, s_rx, s_yr, s_ya, s_ag, s_fw,
    s_snd, s_mr, s_ms, s_mix, s_mixs, s_g, s_gs, s_gl,
):
    row, col = lax.axis_index("row"), lax.axis_index("col")
    x, yh, core = row // 4, (row // 2) % 2, row % 2
    yl, z = col // 8, col % 8

    def dev(x=x, yh=yh, core=core, yl=yl, z=z):
        return ((x * 2 + yh) * 2 + core, yl * 8 + z)

    right, left, across = (x + 1) % 4, (x + 3) % 4, (x + 2) % 4
    east, west = dev(x=right), dev(x=left)
    twin = dev(core=1 - core)
    pair = dev(yh=1 - yh)
    beside = dev(yl=1 - yl)
    up, down = dev(z=(z + 1) % 8), dev(z=(z + 7) % 8)

    barrier = pltpu.get_barrier_semaphore()
    for peer in (east, west, twin, pair):
        pl.semaphore_signal(barrier, inc=1, device_id=peer, device_id_type=MESH)
    for step in range(1, 16):
        pl.semaphore_signal(
            barrier, inc=1, device_id=(row, (col + step) % 16), device_id_type=MESH
        )

    def send(src, dst, send_sem, recv_sem, to):
        pltpu.make_async_remote_copy(
            src_ref=src, dst_ref=dst, send_sem=send_sem, recv_sem=recv_sem,
            device_id=to, device_id_type=MESH,
        ).start()

    def wait(ref, sem):
        pltpu.make_async_copy(ref, ref, sem).wait()

    def ds(start, size):
        return pl.ds(pl.multiple_of(start, size), size)

    mine = ds(core * WIDE, WIDE)
    other = ds((1 - core) * WIDE, WIDE)
    own, far = pl.ds(0, FEAT), pl.ds(FEAT, FEAT)
    s0, s1 = pl.ds(0, TOK), pl.ds(TOK, TOK)

    local = [
        pltpu.make_async_copy(lat, X.at[0, s0, own], s_loc.at[0]),
        pltpu.make_async_copy(w_in.at[:, mine], WI.at[own], s_loc.at[1]),
        pltpu.make_async_copy(w_out.at[mine], WO.at[:, own], s_loc.at[2]),
        pltpu.make_async_copy(cot, X.at[8, s0, own], s_loc.at[3]),
    ]
    for c in local:
        c.start()

    pl.semaphore_wait(barrier, 19)

    def first(src, j):
        send(src, X.at[j, s0, far], s_cs.at[j], s_c.at[j], twin)
        send(src, X.at[j, s1, own], s_xs.at[j], s_x.at[j], beside)
        send(src, X.at[j + 1, s0, own], s_xs.at[j], s_x.at[j + 1], up)
        send(src, X.at[j + 2, s0, own], s_xs.at[j], s_x.at[j + 2], down)

    def second(j):
        block = X.at[j, s1, own]
        wait(block, s_x.at[j])
        send(block, X.at[j + 1, s1, own], s_xs.at[j], s_x.at[j + 1], up)
        send(block, X.at[j + 2, s1, own], s_xs.at[j], s_x.at[j + 2], down)
        send(block, X.at[j, s1, far], s_cs.at[j], s_c.at[j], twin)

    first(lat, 0)
    send(w_in.at[:, other], WI.at[far], s_ws.at[0], s_w.at[0], twin)
    send(w_out.at[other], WO.at[:, far], s_ws.at[1], s_w.at[1], twin)
    second(0)
    for c in local:
        c.wait()
    wait(WI.at[own], s_w.at[0])
    wait(WO.at[:, own], s_w.at[1])

    def gather(j):
        k = j % CH
        whole = X.at[j, :, own]
        wait(whole, s_x.at[j])
        send(whole, X.at[j, :, far], s_cs.at[j], s_c.at[j], twin)
        onward = dev(z=(z + 1 + (1 - k % 2) * 6) % 8)

        @pl.when(k <= 4)
        def _():
            send(whole, X.at[j + 2, :, own], s_xs.at[j], s_x.at[j + 2], onward)

        @pl.when(k == 5)
        def _():
            send(X.at[j, s0, own], X.at[j + 2, s0, own], s_xs.at[j], s_x.at[j + 2], onward)

        @pl.when(k == 6)
        def _():
            send(X.at[j, s1, own], X.at[j + 1, s1, own], s_xs.at[j], s_x.at[j + 1], onward)

    def part(j):
        wait(X.at[j, :, own], s_c.at[j])

        @pl.when(j < CH)
        def _():
            PT[j] = dot(X[j], WI[...], NN).astype(BF)

        @pl.when(j >= CH)
        def _():
            PT[j] = dot(X[j], WO[...], NT).astype(BF)

        ss = s_snd.at[j]
        send(PT.at[j, ds(across * PIECE, HALF)], FAR.at[j, 0], ss, s_far.at[j], east)
        send(PT.at[j, ds(across * PIECE + HALF, HALF)], FAR.at[j, 1], ss, s_far.at[j], west)
        send(PT.at[j, ds(right * PIECE + HALF, HALF)], RX.at[j, 0, pl.ds(HALF, HALF)], ss, s_rx.at[j], east)
        send(PT.at[j, ds(left * PIECE, HALF)], RX.at[j, 1, pl.ds(0, HALF)], ss, s_rx.at[j], west)

    def combine(j):
        wait(FAR.at[j], s_far.at[j])
        ss = s_snd.at[j]
        a = PT[j, ds(right * PIECE, HALF), :].astype(F32) + FAR[j, 0].astype(F32)
        CMB[j, 0] = a.astype(BF)
        b = PT[j, ds(left * PIECE + HALF, HALF), :].astype(F32) + FAR[j, 1].astype(F32)
        CMB[j, 1] = b.astype(BF)
        send(CMB.at[j, 0], RX.at[j, 0, pl.ds(0, HALF)], ss, s_rx.at[j], east)
        send(CMB.at[j, 1], RX.at[j, 1, pl.ds(HALF, HALF)], ss, s_rx.at[j], west)

    def total(j):
        wait(RX.at[j], s_rx.at[j])

        def summed(which):
            t = PT[j, ds(x * PIECE + which * HALF, HALF), :].astype(F32)
            t = t + RX[j, 0, ds(which * HALF, HALF), :].astype(F32)
            return t + RX[j, 1, ds(which * HALF, HALF), :].astype(F32)

        YS[j] = summed(1 - yh).astype(BF)
        send(YS.at[j], YR.at[j], s_snd.at[j], s_yr.at[j], pair)
        HS[j] = summed(yh)

    def point(j):
        wait(YR.at[j], s_yr.at[j])
        h = HS[j] + YR[j].astype(F32)
        here = ds(x * PIECE + yh * HALF, HALF)

        @pl.when(j < CH)
        def _():
            cdf = 0.5 * (1.0 + lax.erf(h * 0.7071067811865476))
            pdf = jnp.exp(-0.5 * h * h) * 0.3989422804014327
            A[j, here, :] = (h * cdf).astype(BF)
            SL[j] = cdf + h * pdf

        @pl.when(j >= CH)
        def _():
            A[j, here, :] = (h * SL[j - CH]).astype(BF)

        block = A.at[j, here]
        send(block, block, s_snd.at[j], s_ya.at[j], pair)

    def spread(j):
        wait(YR.at[j], s_ya.at[j])
        block = A.at[j, ds(x * PIECE, PIECE)]
        send(block, block, s_snd.at[j], s_ag.at[j], east)
        send(block, block, s_snd.at[j], s_ag.at[j], west)

    def onward(j):
        wait(RX.at[j], s_ag.at[j])
        a = A.at[j, ds(left * PIECE, HALF)]
        b = A.at[j, ds(right * PIECE + HALF, HALF)]
        send(a, a, s_snd.at[j], s_fw.at[j], east)
        send(b, b, s_snd.at[j], s_fw.at[j], west)

    def use(j):
        wait(FAR.at[j], s_fw.at[j])

        @pl.when(j < CH)
        def _():
            m = dot(A[j], WO[...], NN)
            MS[j] = m[:, FEAT:].astype(BF)
            send(MS.at[j], MR.at[j], s_ms.at[j], s_mr.at[j], twin)
            MO[j] = m[:, :FEAT]

        @pl.when(j >= CH)
        def _():
            GW[1] = GW[1] + dot(X[j - CH], A[j], TN)

    def use_late(j):
        GW[0] = GW[0] + dot(A[j], X[j + CH], TN)

        @pl.when(j == CH - 1)
        def _():
            GB[0] = GW[0].astype(BF)
            pltpu.make_async_copy(GB.at[0, :, own], g_out.at[mine], s_gl.at[0]).start()
            send(GB.at[0, :, far], g_out.at[mine], s_gs.at[0], s_g.at[0], twin)

    def mix(j):
        wait(MS.at[j], s_mr.at[j])
        MT[j] = (MO[j] + MR[j].astype(F32)).astype(BF)
        there = (z + j // 2 + 8 - (j % 2) * j) % 8

        @pl.when(j > 0)
        def _():
            send(MT.at[j, s0], MIX.at[2 * j - 1], s_mixs.at[j], s_mix, dev(z=there))

        send(MT.at[j, s1], MIX.at[2 * j], s_mixs.at[j], s_mix, dev(yl=1 - yl, z=there))

    GW[...] = jnp.zeros_like(GW)

    def stage(f, j, lo=0, hi=16):
        @pl.when((j >= lo) & (j < hi))
        def _():
            f(j)

    def step(i, carry):
        stage(combine, i - 2)
        stage(total, i - 3)
        stage(point, i - 4)
        stage(spread, i - 5)
        stage(onward, i - 6)

        @pl.when((i > 0) & (i < 16) & (i != CH))
        def _():
            gather(i)

        stage(part, i - 1)
        stage(mix, i - 8, 0, CH)
        stage(use, i - 7)
        stage(use_late, i - 9, 0, CH)

        @pl.when(i == 2)
        def _():
            first(cot, CH)

        @pl.when(i == 4)
        def _():
            second(CH)

        return carry

    lax.fori_loop(0, 23, step, 0)

    GB[1] = GW[1].astype(BF)
    send(GB.at[1, far], g_in.at[:, mine], s_gs.at[1], s_g.at[1], twin)
    last = pltpu.make_async_copy(GB.at[1, own], g_in.at[:, mine], s_gl.at[1])
    last.start()

    wait(MIX, s_mix)
    t = MT[0, :TOK, :].astype(F32)
    for k in range(15):
        t = t + MIX[k].astype(F32)
    OUT[...] = t.astype(BF)
    done = pltpu.make_async_copy(OUT, mixed, s_gl.at[2])
    done.start()

    wait(WI.at[own], s_ws.at[0])
    wait(WO.at[:, own], s_ws.at[1])

    def drain(j, carry):
        k = j % CH
        wait(A.at[pl.ds(0, 7), pl.ds(0, PIECE)], s_snd.at[j])
        wait(X.at[j, :, own], s_cs.at[j])

        @pl.when(k == 0)
        def _():
            wait(MIX.at[pl.ds(0, 5)], s_xs.at[j])

        @pl.when((k > 0) & (k <= 4))
        def _():
            wait(X.at[j, :, own], s_xs.at[j])

        @pl.when((k == 5) | (k == 6))
        def _():
            wait(X.at[j, s0, own], s_xs.at[j])

        @pl.when(j < CH)
        def _():
            wait(MS.at[j], s_ms.at[j])

        @pl.when((j < CH) & (j > 0))
        def _():
            wait(MT.at[j], s_mixs.at[j])

        @pl.when(j == 0)
        def _():
            wait(MT.at[j, s1], s_mixs.at[j])

        return carry

    lax.fori_loop(0, 16, drain, 0)
    for i, (ref, half) in enumerate(((g_out.at[mine], GB.at[0, :, own]), (g_in.at[:, mine], GB.at[1, own]))):
        wait(half, s_gs.at[i])
        wait(half, s_g.at[i])
        wait(half, s_gl.at[i])
    done.wait()


def per_device(latents, w_in, w_out, cotangent):
    anyspec = pl.BlockSpec(memory_space=pl.ANY)
    V, D = pltpu.VMEM, pltpu.SemaphoreType.DMA
    return pl.pallas_call(
        kernel,
        out_shape=(
            jax.ShapeDtypeStruct((TOK, FEAT), BF),
            jax.ShapeDtypeStruct((FEAT, HID), BF),
            jax.ShapeDtypeStruct((HID, FEAT), BF),
        ),
        in_specs=[anyspec] * 4,
        out_specs=[anyspec] * 3,
        scratch_shapes=[
            V((16, ROWS, WIDE), BF),
            V((WIDE, WIDE), BF),
            V((WIDE, WIDE), BF),
            V((16, ROWS, WIDE), BF),
            V((16, 2, HALF, WIDE), BF),
            V((16, 2, HALF, WIDE), BF),
            V((16, 2, PIECE, WIDE), BF),
            V((16, HALF, WIDE), BF),
            V((16, HALF, WIDE), BF),
            V((16, HALF, WIDE), F32),
            V((CH, HALF, WIDE), F32),
            V((16, ROWS, WIDE), BF),
            V((CH, ROWS, FEAT), F32),
            V((CH, ROWS, FEAT), BF),
            V((CH, ROWS, FEAT), BF),
            V((CH, ROWS, FEAT), BF),
            V((15, TOK, FEAT), BF),
            V((TOK, FEAT), BF),
            V((2, WIDE, WIDE), F32),
            V((2, WIDE, WIDE), BF),
            D((4,)),
            D((2,)),
            D((2,)),
            D((16,)),
            D((16,)),
            D((16,)),
            D((16,)),
            D((16,)),
            D((16,)),
            D((16,)),
            D((16,)),
            D((16,)),
            D((16,)),
            D((16,)),
            D((CH,)),
            D((CH,)),
            D,
            D((CH,)),
            D((2,)),
            D((2,)),
            D((3,)),
        ],
        compiler_params=pltpu.CompilerParams(
            collective_id=0, has_side_effects=True, vmem_limit_bytes=62 * 1024 * 1024
        ),
        cost_estimate=pl.CostEstimate(
            flops=12 * 10**9, bytes_accessed=5 * 10**6, transcendentals=10**6
        ),
    )(latents, w_in, w_out, cotangent)


def solution(mesh):
    placed = (P("col", "row"), P("row", "col"), P("col", "row"), P("col", "row"))
    return jax.shard_map(
        per_device,
        mesh=mesh,
        in_specs=placed,
        out_specs=(P("col", "row"), P("row", "col"), P("col", "row")),
        check_vma=False,
    )
```

```python
import jax
import jax.numpy as jnp
from jax import lax
from jax.experimental import pallas as pl
from jax.experimental.pallas import tpu as pltpu
from jax.sharding import PartitionSpec as P

MESH = pl.DeviceIdType.MESH
BF = jnp.bfloat16
F32 = jnp.float32

TOK, FEAT, HID = 128, 384, 1536
ROWS, WIDE = 256, 768
CH = 8
LAG = 2
PIECE, HALF = 64, 32

NN = (((1,), (0,)), ((), ()))
NT = (((1,), (1,)), ((), ()))
TN = (((0,), (0,)), ((), ()))


def dot(a, b, dims):
    return lax.dot_general(a, b, dims, preferred_element_type=F32)


def kernel(
    lat, w_in, w_out, cot,
    mixed, g_in, g_out,
    X, WI, WO, PT, FAR, CMB, RX, YS, YR, HS, SL, A, MO, MS, MR, MT, MIX, OUT, GW, GB,
    s_loc, s_w, s_ws, s_x, s_xs, s_c, s_cs, s_far, s_rx, s_yr, s_ya, s_ag, s_fw,
    s_snd, s_mr, s_ms, s_mix, s_mixs, s_g, s_gs, s_gl,
):
    row, col = lax.axis_index("row"), lax.axis_index("col")
    x, yh, core = row // 4, (row // 2) % 2, row % 2
    yl, z = col // 8, col % 8

    def dev(x=x, yh=yh, core=core, yl=yl, z=z):
        return ((x * 2 + yh) * 2 + core, yl * 8 + z)

    right, left, across = (x + 1) % 4, (x + 3) % 4, (x + 2) % 4
    east, west = dev(x=right), dev(x=left)
    twin = dev(core=1 - core)
    pair = dev(yh=1 - yh)
    beside = dev(yl=1 - yl)
    up, down = dev(z=(z + 1) % 8), dev(z=(z + 7) % 8)

    barrier = pltpu.get_barrier_semaphore()
    for peer in (east, west, twin, pair):
        pl.semaphore_signal(barrier, inc=1, device_id=peer, device_id_type=MESH)
    for step in range(1, 16):
        pl.semaphore_signal(
            barrier, inc=1, device_id=(row, (col + step) % 16), device_id_type=MESH
        )

    def send(src, dst, send_sem, recv_sem, to):
        pltpu.make_async_remote_copy(
            src_ref=src, dst_ref=dst, send_sem=send_sem, recv_sem=recv_sem,
            device_id=to, device_id_type=MESH,
        ).start()

    def wait(ref, sem):
        pltpu.make_async_copy(ref, ref, sem).wait()

    def ds(start, size):
        return pl.ds(pl.multiple_of(start, size), size)

    mine = ds(core * WIDE, WIDE)
    other = ds((1 - core) * WIDE, WIDE)
    own, far = pl.ds(0, FEAT), pl.ds(FEAT, FEAT)
    s0, s1 = pl.ds(0, TOK), pl.ds(TOK, TOK)

    local = [
        pltpu.make_async_copy(lat, X.at[0, s0, own], s_loc.at[0]),
        pltpu.make_async_copy(w_in.at[:, mine], WI.at[own], s_loc.at[1]),
        pltpu.make_async_copy(w_out.at[mine], WO.at[:, own], s_loc.at[2]),
        pltpu.make_async_copy(cot, X.at[8, s0, own], s_loc.at[3]),
    ]
    for c in local:
        c.start()

    pl.semaphore_wait(barrier, 19)

    def first(src, j):
        send(src, X.at[j, s0, far], s_cs.at[j], s_c.at[j], twin)
        send(src, X.at[j, s1, own], s_xs.at[j], s_x.at[j], beside)
        send(src, X.at[j + 1, s0, own], s_xs.at[j], s_x.at[j + 1], up)
        send(src, X.at[j + 1, s1, own], s_xs.at[j], s_x.at[j + 1], down)

    def second(j):
        block = X.at[j, s1, own]
        wait(block, s_x.at[j])
        send(block, X.at[j + 2, s0, own], s_xs.at[j], s_x.at[j + 2], up)
        send(block, X.at[j + 2, s1, own], s_xs.at[j], s_x.at[j + 2], down)
        send(block, X.at[j, s1, far], s_cs.at[j], s_c.at[j], twin)

    first(lat, 0)
    send(w_in.at[:, other], WI.at[far], s_ws.at[0], s_w.at[0], twin)
    send(w_out.at[other], WO.at[:, far], s_ws.at[1], s_w.at[1], twin)
    second(0)
    for c in local:
        c.wait()
    wait(WI.at[own], s_w.at[0])
    wait(WO.at[:, own], s_w.at[1])

    def gather(j):
        k = j % CH
        whole = X.at[j, :, own]
        wait(whole, s_x.at[j])
        send(whole, X.at[j, :, far], s_cs.at[j], s_c.at[j], twin)
        low, high = X.at[j, s0, own], X.at[j, s1, own]

        @pl.when(k <= 5)
        def _():
            send(low, X.at[j + 2, s0, own], s_xs.at[j], s_x.at[j + 2], up)

        @pl.when(k <= 4)
        def _():
            send(high, X.at[j + 2, s1, own], s_xs.at[j], s_x.at[j + 2], down)

        @pl.when(k == 6)
        def _():
            send(high, X.at[j + 1, s1, own], s_xs.at[j], s_x.at[j + 1], down)

    def part(j):
        wait(X.at[j, :, own], s_c.at[j])

        @pl.when(j < CH)
        def _():
            PT[j] = dot(X[j], WI[...], NN).astype(BF)

        @pl.when(j >= CH)
        def _():
            PT[j] = dot(X[j], WO[...], NT).astype(BF)

        ss = s_snd.at[j]
        send(PT.at[j, ds(across * PIECE, HALF)], FAR.at[j, 0], ss, s_far.at[j], east)
        send(PT.at[j, ds(across * PIECE + HALF, HALF)], FAR.at[j, 1], ss, s_far.at[j], west)
        send(PT.at[j, ds(right * PIECE + HALF, HALF)], RX.at[j, 0, pl.ds(HALF, HALF)], ss, s_rx.at[j], east)
        send(PT.at[j, ds(left * PIECE, HALF)], RX.at[j, 1, pl.ds(0, HALF)], ss, s_rx.at[j], west)

    def combine(j):
        wait(FAR.at[j], s_far.at[j])
        ss = s_snd.at[j]
        a = PT[j, ds(right * PIECE, HALF), :].astype(F32) + FAR[j, 0].astype(F32)
        CMB[j, 0] = a.astype(BF)
        b = PT[j, ds(left * PIECE + HALF, HALF), :].astype(F32) + FAR[j, 1].astype(F32)
        CMB[j, 1] = b.astype(BF)
        send(CMB.at[j, 0], RX.at[j, 0, pl.ds(0, HALF)], ss, s_rx.at[j], east)
        send(CMB.at[j, 1], RX.at[j, 1, pl.ds(HALF, HALF)], ss, s_rx.at[j], west)

    def total(j):
        wait(RX.at[j], s_rx.at[j])

        def summed(which):
            t = PT[j, ds(x * PIECE + which * HALF, HALF), :].astype(F32)
            t = t + RX[j, 0, ds(which * HALF, HALF), :].astype(F32)
            return t + RX[j, 1, ds(which * HALF, HALF), :].astype(F32)

        YS[j] = summed(1 - yh).astype(BF)
        send(YS.at[j], YR.at[j], s_snd.at[j], s_yr.at[j], pair)
        HS[j] = summed(yh)

    def point(j):
        wait(YR.at[j], s_yr.at[j])
        h = HS[j] + YR[j].astype(F32)
        here = ds(x * PIECE + yh * HALF, HALF)

        @pl.when(j < CH)
        def _():
            cdf = 0.5 * (1.0 + lax.erf(h * 0.7071067811865476))
            pdf = jnp.exp(-0.5 * h * h) * 0.3989422804014327
            A[j, here, :] = (h * cdf).astype(BF)
            SL[j] = cdf + h * pdf

        @pl.when(j >= CH)
        def _():
            A[j, here, :] = (h * SL[j - CH]).astype(BF)

        block = A.at[j, here]
        send(block, block, s_snd.at[j], s_ya.at[j], pair)

    def spread(j):
        wait(YR.at[j], s_ya.at[j])
        block = A.at[j, ds(x * PIECE, PIECE)]
        send(block, block, s_snd.at[j], s_ag.at[j], east)
        send(block, block, s_snd.at[j], s_ag.at[j], west)

    def onward(j):
        wait(RX.at[j], s_ag.at[j])
        a = A.at[j, ds(left * PIECE, HALF)]
        b = A.at[j, ds(right * PIECE + HALF, HALF)]
        send(a, a, s_snd.at[j], s_fw.at[j], east)
        send(b, b, s_snd.at[j], s_fw.at[j], west)

    def use(j):
        wait(FAR.at[j], s_fw.at[j])

        @pl.when(j < CH)
        def _():
            m = dot(A[j], WO[...], NN)
            MS[j] = m[:, FEAT:].astype(BF)
            send(MS.at[j], MR.at[j], s_ms.at[j], s_mr.at[j], twin)
            MO[j] = m[:, :FEAT]
            GW[0] = GW[0] + dot(A[j], X[j + CH], TN)

        @pl.when(j >= CH)
        def _():
            GW[1] = GW[1] + dot(X[j - CH], A[j], TN)

        @pl.when(j == CH - 1)
        def _():
            GB[0] = GW[0].astype(BF)
            pltpu.make_async_copy(GB.at[0, :, own], g_out.at[mine], s_gl.at[0]).start()
            send(GB.at[0, :, far], g_out.at[mine], s_gs.at[0], s_g.at[0], twin)

    def mix(j):
        wait(MS.at[j], s_mr.at[j])
        MT[j] = (MO[j] + MR[j].astype(F32)).astype(BF)
        m = (j + 1) // 2
        below, above = (z + 8 - m) % 8, (z + m) % 8
        low, high = MT.at[j, s0], MT.at[j, s1]
        sems = s_mixs.at[j], s_mix

        @pl.when((j > 0) & (j < CH - 1))
        def _():
            line = (yl + j + 1) % 2
            send(low, MIX.at[2 * j - 1], *sems, dev(yl=line, z=below))
            send(high, MIX.at[2 * j], *sems, dev(yl=line, z=above))

        @pl.when(j == CH - 1)
        def _():
            send(low, MIX.at[2 * j - 1], *sems, dev(z=above))

        @pl.when((j == 0) | (j == CH - 1))
        def _():
            send(high, MIX.at[2 * j], *sems, dev(yl=1 - yl, z=above))

    GW[...] = jnp.zeros_like(GW)

    def reduce_stage(f, t):
        @pl.when((t >= 0) & (t < CH))
        def _():
            f(t)

        @pl.when((t >= CH) & (t < 3 * CH) & (t % 2 == 0))
        def _():
            f(t // 2 + CH // 2)

    def spread_stage(f, t):
        @pl.when((t > CH) & (t < 3 * CH) & (t % 2 == 1))
        def _():
            f((t - CH) // 2)

        @pl.when((t >= 3 * CH) & (t < 4 * CH))
        def _():
            f(t - 2 * CH)

    def step(t, carry):
        spread_stage(onward, t - LAG)
        spread_stage(spread, t)
        reduce_stage(point, t - 3 * LAG)
        reduce_stage(total, t - 2 * LAG)
        reduce_stage(combine, t - LAG)

        @pl.when((t >= 0) & (t < CH - 1))
        def _():
            gather(t + 1)

        @pl.when((t >= CH) & (t < 3 * CH - 2) & (t % 2 == 0))
        def _():
            gather(t // 2 + CH // 2 + 1)

        reduce_stage(part, t)

        @pl.when((t - 2 * LAG - 1 > CH) & (t - 2 * LAG - 1 < 3 * CH) & ((t - 2 * LAG - 1) % 2 == 1))
        def _():
            mix((t - 2 * LAG - 1 - CH) // 2)

        spread_stage(use, t - 2 * LAG)

        @pl.when(t == 3)
        def _():
            first(cot, CH)

        @pl.when(t == 6)
        def _():
            second(CH)

        return carry

    lax.fori_loop(0, 4 * CH + 2 * LAG, step, 0)

    GB[1] = GW[1].astype(BF)
    send(GB.at[1, far], g_in.at[:, mine], s_gs.at[1], s_g.at[1], twin)
    last = pltpu.make_async_copy(GB.at[1, own], g_in.at[:, mine], s_gl.at[1])
    last.start()

    wait(MIX, s_mix)
    t = MT[0, :TOK, :].astype(F32)
    for k in range(15):
        t = t + MIX[k].astype(F32)
    OUT[...] = t.astype(BF)
    done = pltpu.make_async_copy(OUT, mixed, s_gl.at[2])
    done.start()

    wait(WI.at[own], s_ws.at[0])
    wait(WO.at[:, own], s_ws.at[1])

    def drain(j, carry):
        k = j % CH
        wait(A.at[pl.ds(0, 7), pl.ds(0, PIECE)], s_snd.at[j])
        wait(X.at[j, :, own], s_cs.at[j])

        @pl.when(k == 0)
        def _():
            wait(MIX.at[pl.ds(0, 5)], s_xs.at[j])

        @pl.when((k > 0) & (k <= 4))
        def _():
            wait(X.at[j, :, own], s_xs.at[j])

        @pl.when((k == 5) | (k == 6))
        def _():
            wait(X.at[j, s0, own], s_xs.at[j])

        @pl.when(j < CH)
        def _():
            wait(MS.at[j], s_ms.at[j])

        @pl.when((j < CH) & (j > 0))
        def _():
            wait(MT.at[j], s_mixs.at[j])

        @pl.when(j == 0)
        def _():
            wait(MT.at[j, s1], s_mixs.at[j])

        return carry

    lax.fori_loop(0, 16, drain, 0)
    for i, (ref, half) in enumerate(((g_out.at[mine], GB.at[0, :, own]), (g_in.at[:, mine], GB.at[1, own]))):
        wait(half, s_gs.at[i])
        wait(half, s_g.at[i])
        wait(half, s_gl.at[i])
    done.wait()


def per_device(latents, w_in, w_out, cotangent):
    anyspec = pl.BlockSpec(memory_space=pl.ANY)
    V, D = pltpu.VMEM, pltpu.SemaphoreType.DMA
    return pl.pallas_call(
        kernel,
        out_shape=(
            jax.ShapeDtypeStruct((TOK, FEAT), BF),
            jax.ShapeDtypeStruct((FEAT, HID), BF),
            jax.ShapeDtypeStruct((HID, FEAT), BF),
        ),
        in_specs=[anyspec] * 4,
        out_specs=[anyspec] * 3,
        scratch_shapes=[
            V((16, ROWS, WIDE), BF),
            V((WIDE, WIDE), BF),
            V((WIDE, WIDE), BF),
            V((16, ROWS, WIDE), BF),
            V((16, 2, HALF, WIDE), BF),
            V((16, 2, HALF, WIDE), BF),
            V((16, 2, PIECE, WIDE), BF),
            V((16, HALF, WIDE), BF),
            V((16, HALF, WIDE), BF),
            V((16, HALF, WIDE), F32),
            V((CH, HALF, WIDE), F32),
            V((16, ROWS, WIDE), BF),
            V((CH, ROWS, FEAT), F32),
            V((CH, ROWS, FEAT), BF),
            V((CH, ROWS, FEAT), BF),
            V((CH, ROWS, FEAT), BF),
            V((15, TOK, FEAT), BF),
            V((TOK, FEAT), BF),
            V((2, WIDE, WIDE), F32),
            V((2, WIDE, WIDE), BF),
            D((4,)),
            D((2,)),
            D((2,)),
            D((16,)),
            D((16,)),
            D((16,)),
            D((16,)),
            D((16,)),
            D((16,)),
            D((16,)),
            D((16,)),
            D((16,)),
            D((16,)),
            D((16,)),
            D((CH,)),
            D((CH,)),
            D,
            D((CH,)),
            D((2,)),
            D((2,)),
            D((3,)),
        ],
        compiler_params=pltpu.CompilerParams(
            collective_id=0, has_side_effects=True, vmem_limit_bytes=62 * 1024 * 1024
        ),
        cost_estimate=pl.CostEstimate(
            flops=12 * 10**9, bytes_accessed=5 * 10**6, transcendentals=10**6
        ),
    )(latents, w_in, w_out, cotangent)


def solution(mesh):
    placed = (P("col", "row"), P("row", "col"), P("col", "row"), P("col", "row"))
    return jax.shard_map(
        per_device,
        mesh=mesh,
        in_specs=placed,
        out_specs=(P("col", "row"), P("row", "col"), P("col", "row")),
        check_vma=False,
    )
```

```python
import jax
import jax.numpy as jnp
from jax import lax
from jax.experimental import pallas as pl
from jax.experimental.pallas import tpu as pltpu
from jax.sharding import PartitionSpec as P

MESH = pl.DeviceIdType.MESH
BF = jnp.bfloat16
F32 = jnp.float32

TOK, FEAT, HID = 128, 384, 1536
ROWS, WIDE = 256, 768
CH = 8
RF0, RF, RB0, RB = 0, 1, 11, 1
GF0, GF, GB0, GB1 = 8, 1, 23, 1
LF, LB, MF, MB = 2, 3, 2, 3
COT = 6, 8
TICKS = GB0 + 7 * GB1 + 2 * MB + 1
BAND, PART, BIT = 128, 32, 16
PIECE, HALF = 64, 32

NN = (((1,), (0,)), ((), ()))
NT = (((1,), (1,)), ((), ()))
TN = (((0,), (0,)), ((), ()))


def dot(a, b, dims):
    return lax.dot_general(a, b, dims, preferred_element_type=F32)


def kernel(
    lat, w_in, w_out, cot,
    mixed, g_in, g_out,
    X, WI, WO, PT, FAR, CMB, RX, YB, YS, YR, SL, A, MO, MS, MR, MT, MIX, SIDE, OUT, GW, GB,
    s_loc, s_w, s_ws, s_x, s_xs, s_c, s_cs, s_far, s_rx, s_yr, s_ya, s_ag, s_fw,
    s_snd, s_mr, s_ms, s_mix, s_mixs, s_side, s_g, s_gs, s_gl,
):
    row, col = lax.axis_index("row"), lax.axis_index("col")
    x, yh, core = row // 4, (row // 2) % 2, row % 2
    yl, z = col // 8, col % 8

    def dev(x=x, yh=yh, core=core, yl=yl, z=z):
        return ((x * 2 + yh) * 2 + core, yl * 8 + z)

    right, left, across = (x + 1) % 4, (x + 3) % 4, (x + 2) % 4
    east, west = dev(x=right), dev(x=left)
    twin = dev(core=1 - core)
    pair = dev(yh=1 - yh)
    beside = dev(yl=1 - yl)
    up, down = dev(z=(z + 1) % 8), dev(z=(z + 7) % 8)

    barrier = pltpu.get_barrier_semaphore()
    peers = [east, west, twin, pair, beside] + [dev(z=(z + i) % 8) for i in range(1, 8)]
    for peer in peers:
        pl.semaphore_signal(barrier, inc=1, device_id=peer, device_id_type=MESH)

    def send(src, dst, send_sem, recv_sem, to):
        pltpu.make_async_remote_copy(
            src_ref=src, dst_ref=dst, send_sem=send_sem, recv_sem=recv_sem,
            device_id=to, device_id_type=MESH,
        ).start()

    def wait(ref, sem):
        pltpu.make_async_copy(ref, ref, sem).wait()

    def ds(start, size):
        return pl.ds(pl.multiple_of(start, size), size)

    mine = ds(core * WIDE, WIDE)
    other = ds((1 - core) * WIDE, WIDE)
    own, far = pl.ds(0, FEAT), pl.ds(FEAT, FEAT)
    s0, s1 = pl.ds(0, TOK), pl.ds(TOK, TOK)

    local = [
        pltpu.make_async_copy(lat, X.at[0, s0, own], s_loc.at[0]),
        pltpu.make_async_copy(w_in.at[:, mine], WI.at[own], s_loc.at[1]),
        pltpu.make_async_copy(w_out.at[mine], WO.at[:, own], s_loc.at[2]),
        pltpu.make_async_copy(cot, X.at[8, s0, own], s_loc.at[3]),
    ]
    for c in local:
        c.start()

    pl.semaphore_wait(barrier, len(peers))

    def first(src, j):
        send(src, X.at[j, s0, far], s_cs.at[j], s_c.at[j], twin)
        send(src, X.at[j, s1, own], s_xs.at[j], s_x.at[j], beside)
        send(src, X.at[j + 1, s0, own], s_xs.at[j], s_x.at[j + 1], up)
        send(src, X.at[j + 1, s1, own], s_xs.at[j], s_x.at[j + 1], down)

    def second(j):
        block = X.at[j, s1, own]
        wait(block, s_x.at[j])
        send(block, X.at[j + 2, s0, own], s_xs.at[j], s_x.at[j + 2], up)
        send(block, X.at[j + 2, s1, own], s_xs.at[j], s_x.at[j + 2], down)
        send(block, X.at[j, s1, far], s_cs.at[j], s_c.at[j], twin)

    first(lat, 0)
    send(w_in.at[:, other], WI.at[far], s_ws.at[0], s_w.at[0], twin)
    send(w_out.at[other], WO.at[:, far], s_ws.at[1], s_w.at[1], twin)
    second(0)
    for c in local:
        c.wait()
    wait(WI.at[own], s_w.at[0])
    wait(WO.at[:, own], s_w.at[1])

    def gather(j, fwd):
        k = j % CH
        whole = X.at[j, :, own]
        wait(whole, s_x.at[j])
        send(whole, X.at[j, :, far], s_cs.at[j], s_c.at[j], twin)
        low, high = X.at[j, s0, own], X.at[j, s1, own]

        @pl.when(k <= 5)
        def _():
            send(low, X.at[j + 2, s0, own], s_xs.at[j], s_x.at[j + 2], up)

        @pl.when(k <= 4)
        def _():
            send(high, X.at[j + 2, s1, own], s_xs.at[j], s_x.at[j + 2], down)

        @pl.when(k == 6)
        def _():
            send(high, X.at[j + 1, s1, own], s_xs.at[j], s_x.at[j + 1], down)

    def x_first(j):
        return (j % 2 == 0) | (j % CH == CH - 1)

    def y_first(j):
        return (j % 2 == 1) & (j % CH != CH - 1)

    def either(f, g):
        def chosen(j, fwd):
            pl.when(x_first(j))(lambda: f(j, fwd))
            pl.when(y_first(j))(lambda: g(j, fwd))

        return chosen

    def pointwise(j, fwd, h, here, rows):
        if fwd:
            cdf = 0.5 * (1.0 + lax.erf(h * 0.7071067811865476))
            pdf = jnp.exp(-0.5 * h * h) * 0.3989422804014327
            A[j, here, :] = (h * cdf).astype(BF)
            SL[j, pl.ds(0, rows), :] = cdf + h * pdf
        else:
            A[j, here, :] = (h * SL[j - CH, pl.ds(0, rows), :]).astype(BF)

    def part(j, fwd):
        wait(X.at[j, :, own], s_c.at[j])

        PT[j] = (dot(X[j], WI[...], NN) if fwd else dot(X[j], WO[...], NT)).astype(BF)
        ss = s_snd.at[j]

        @pl.when(x_first(j))
        def _():
            send(PT.at[j, ds(across * PIECE, HALF)], FAR.at[j, 0], ss, s_far.at[j], east)
            send(PT.at[j, ds(across * PIECE + HALF, HALF)], FAR.at[j, 1], ss, s_far.at[j], west)
            send(PT.at[j, ds(right * PIECE + HALF, HALF)], RX.at[j, 0, pl.ds(HALF, HALF)], ss, s_rx.at[j], east)
            send(PT.at[j, ds(left * PIECE, HALF)], RX.at[j, 1, pl.ds(0, HALF)], ss, s_rx.at[j], west)

        @pl.when(y_first(j))
        def _():
            send(PT.at[j, ds((1 - yh) * BAND, BAND)], YB.at[j // 2], ss, s_yr.at[j], pair)

    def combine(j, fwd):
        wait(FAR.at[j], s_far.at[j])
        ss = s_snd.at[j]
        a = PT[j, ds(right * PIECE, HALF), :].astype(F32) + FAR[j, 0].astype(F32)
        CMB[j, 0] = a.astype(BF)
        b = PT[j, ds(left * PIECE + HALF, HALF), :].astype(F32) + FAR[j, 1].astype(F32)
        CMB[j, 1] = b.astype(BF)
        send(CMB.at[j, 0], RX.at[j, 0, pl.ds(0, HALF)], ss, s_rx.at[j], east)
        send(CMB.at[j, 1], RX.at[j, 1, pl.ds(HALF, HALF)], ss, s_rx.at[j], west)

    def total(j, fwd):
        wait(RX.at[j], s_rx.at[j])
        t = PT[j, ds(x * PIECE, PIECE), :].astype(F32)
        YS[j] = (t + RX[j, 0].astype(F32) + RX[j, 1].astype(F32)).astype(BF)
        send(YS.at[j], YR.at[j], s_snd.at[j], s_yr.at[j], pair)

    def spread(j, fwd):
        wait(YR.at[j], s_yr.at[j])
        here = ds(x * PIECE, PIECE)
        pointwise(j, fwd, YS[j].astype(F32) + YR[j].astype(F32), here, PIECE)
        block = A.at[j, here]
        send(block, block, s_snd.at[j], s_ag.at[j], east)
        send(block, block, s_snd.at[j], s_ag.at[j], west)

    def onward(j, fwd):
        wait(RX.at[j], s_ag.at[j])
        a = A.at[j, ds(left * PIECE, HALF)]
        b = A.at[j, ds(right * PIECE + HALF, HALF)]
        send(a, a, s_snd.at[j], s_fw.at[j], east)
        send(b, b, s_snd.at[j], s_fw.at[j], west)

    band = yh * BAND

    def fold(j, fwd):
        wait(YB.at[j // 2], s_yr.at[j])
        rows = ds(band, BAND)
        PT[j, rows, :] = (PT[j, rows, :].astype(F32) + YB[j // 2].astype(F32)).astype(BF)
        ss = s_snd.at[j]
        lo, hi = pl.ds(0, BIT), pl.ds(BIT, BIT)
        send(PT.at[j, ds(band + across * PART, BIT)], FAR.at[j, 0, lo], ss, s_far.at[j], east)
        send(PT.at[j, ds(band + across * PART + BIT, BIT)], FAR.at[j, 1, lo], ss, s_far.at[j], west)
        send(PT.at[j, ds(band + right * PART + BIT, BIT)], RX.at[j, 0, hi], ss, s_rx.at[j], east)
        send(PT.at[j, ds(band + left * PART, BIT)], RX.at[j, 1, lo], ss, s_rx.at[j], west)

    def combine_y(j, fwd):
        wait(FAR.at[j, 0], s_far.at[j])
        ss = s_snd.at[j]
        lo, hi = pl.ds(0, BIT), pl.ds(BIT, BIT)
        a = PT[j, ds(band + right * PART, BIT), :].astype(F32) + FAR[j, 0, lo, :].astype(F32)
        CMB[j, 0, lo, :] = a.astype(BF)
        b = PT[j, ds(band + left * PART + BIT, BIT), :].astype(F32) + FAR[j, 1, lo, :].astype(F32)
        CMB[j, 1, lo, :] = b.astype(BF)
        send(CMB.at[j, 0, lo], RX.at[j, 0, lo], ss, s_rx.at[j], east)
        send(CMB.at[j, 1, lo], RX.at[j, 1, hi], ss, s_rx.at[j], west)

    def point_y(j, fwd):
        wait(RX.at[j, 0], s_rx.at[j])
        here = ds(band + x * PART, PART)
        h = PT[j, here, :].astype(F32) + RX[j, 0, pl.ds(0, PART), :].astype(F32)
        pointwise(j, fwd, h + RX[j, 1, pl.ds(0, PART), :].astype(F32), here, PART)
        block = A.at[j, here]
        send(block, block, s_snd.at[j], s_ag.at[j], east)
        send(block, block, s_snd.at[j], s_ag.at[j], west)

    def onward_y(j, fwd):
        wait(RX.at[j, 0], s_ag.at[j])
        a = A.at[j, ds(band + left * PART, BIT)]
        b = A.at[j, ds(band + right * PART + BIT, BIT)]
        send(a, a, s_snd.at[j], s_fw.at[j], east)
        send(b, b, s_snd.at[j], s_fw.at[j], west)

    def spread_y(j, fwd):
        wait(YR.at[j, pl.ds(0, PART)], s_fw.at[j])
        block = A.at[j, ds(band, BAND)]
        send(block, block, s_snd.at[j], s_ya.at[j], pair)

    def use(j, fwd):
        either(
            lambda j, fwd: wait(FAR.at[j], s_fw.at[j]),
            lambda j, fwd: wait(RX.at[j], s_ya.at[j]),
        )(j, fwd)
        if not fwd:
            GW[1] = GW[1] + dot(X[j - CH], A[j], TN)
            return

        m = dot(A[j], WO[...], NN)
        MS[j] = m[:, FEAT:].astype(BF)
        send(MS.at[j], MR.at[j], s_ms.at[j], s_mr.at[j], twin)
        MO[j] = m[:, :FEAT]
        GW[0] = GW[0] + dot(A[j], X[j + CH], TN)

        @pl.when(j == CH - 1)
        def _():
            GB[0] = GW[0].astype(BF)
            pltpu.make_async_copy(GB.at[0, :, own], g_out.at[mine], s_gl.at[0]).start()
            send(GB.at[0, :, far], g_out.at[mine], s_gs.at[0], s_g.at[0], twin)

    def mix(j, fwd):
        wait(MS.at[j], s_mr.at[j])
        MT[j] = (MO[j] + MR[j].astype(F32)).astype(BF)
        m = (j + 1) // 2
        below, above = (z + 8 - m) % 8, (z + m) % 8
        low, high = MT.at[j, s0], MT.at[j, s1]
        sems = s_mixs.at[j], s_mix

        @pl.when((j > 0) & (j < CH - 1))
        def _():
            line = (j + 1) % 2
            send(low, MIX.at[line, j - line - 1], *sems, dev(z=below))
            send(high, MIX.at[line, j - line], *sems, dev(z=above))

        @pl.when(j == CH - 1)
        def _():
            send(low, MIX.at[0, 6], *sems, dev(z=above))
            send(high, MIX.at[1, 6], *sems, dev(z=above))

    GW[...] = jnp.zeros_like(GW)

    def stage(f, t, fwd, start, step):
        t = t - start
        due = (t >= 0) & (t < 8 * step) & (t % step == 0)
        pl.when(due)(lambda: f(t // step + (0 if fwd else CH), fwd))

    def reduce_stage(f, t, lags):
        stage(f, t - lags * LF, True, RF0, RF)
        stage(f, t - lags * LB, False, RB0, RB)

    def spread_stage(f, t, lags):
        stage(f, t - lags * MF, True, GF0, GF)
        stage(f, t - lags * MB, False, GB0, GB1)

    def idle(j, fwd):
        pass

    def next_gather(j, fwd):
        pl.when(j % CH != CH - 1)(lambda: gather(j + 1, fwd))

    def line_total(line):
        t = MT[0, pl.ds(line * TOK, TOK), :].astype(F32)
        for k in range(7):
            t = t + MIX[line, k].astype(F32)
        return t

    def finish_other():
        wait(MIX, s_mix)
        SIDE[0] = line_total(1).astype(BF)
        send(SIDE.at[0], SIDE.at[1], s_side.at[0], s_side.at[1], beside)

    def finish_own():
        t = line_total(0)
        wait(SIDE.at[1], s_side.at[1])
        OUT[...] = (t + SIDE[1].astype(F32)).astype(BF)
        pltpu.make_async_copy(OUT, mixed, s_gl.at[2]).start()

    def step(t, carry):
        reduce_stage(next_gather, t, 0)
        reduce_stage(part, t, 0)
        spread_stage(either(onward, spread_y), t, 1)
        spread_stage(either(spread, onward_y), t, 0)
        reduce_stage(either(idle, point_y), t, 3)
        reduce_stage(either(total, combine_y), t, 2)
        reduce_stage(either(combine, fold), t, 1)
        stage(mix, t - 2 * MF - 1, True, GF0, GF)
        spread_stage(use, t, 2)

        pl.when(t == TICKS - 3)(finish_other)

        @pl.when(t == COT[0])
        def _():
            first(cot, CH)

        @pl.when(t == COT[1])
        def _():
            second(CH)

        return carry

    lax.fori_loop(0, TICKS, step, 0)

    GB[1] = GW[1].astype(BF)
    send(GB.at[1, far], g_in.at[:, mine], s_gs.at[1], s_g.at[1], twin)
    last = pltpu.make_async_copy(GB.at[1, own], g_in.at[:, mine], s_gl.at[1])
    last.start()

    finish_own()

    wait(WI.at[own], s_ws.at[0])
    wait(WO.at[:, own], s_ws.at[1])

    def drain(j, carry):
        k = j % CH
        wait(A.at[pl.ds(0, 7), pl.ds(0, PIECE)], s_snd.at[j])
        wait(X.at[j, :, own], s_cs.at[j])

        @pl.when(k == 0)
        def _():
            wait(MIX.at[0, pl.ds(0, 5)], s_xs.at[j])

        @pl.when((k > 0) & (k <= 4))
        def _():
            wait(X.at[j, :, own], s_xs.at[j])

        @pl.when((k == 5) | (k == 6))
        def _():
            wait(X.at[j, s0, own], s_xs.at[j])

        @pl.when(j < CH)
        def _():
            wait(MS.at[j], s_ms.at[j])

        @pl.when((j < CH) & (j > 0))
        def _():
            wait(MT.at[j], s_mixs.at[j])

        return carry

    lax.fori_loop(0, 16, drain, 0)
    for i, (ref, half) in enumerate(((g_out.at[mine], GB.at[0, :, own]), (g_in.at[:, mine], GB.at[1, own]))):
        wait(half, s_gs.at[i])
        wait(half, s_g.at[i])
        wait(half, s_gl.at[i])
    wait(SIDE.at[0], s_side.at[0])
    wait(OUT, s_gl.at[2])


def per_device(latents, w_in, w_out, cotangent):
    anyspec = pl.BlockSpec(memory_space=pl.ANY)
    V, D = pltpu.VMEM, pltpu.SemaphoreType.DMA
    return pl.pallas_call(
        kernel,
        out_shape=(V((TOK, FEAT), BF), V((FEAT, HID), BF), V((HID, FEAT), BF)),
        in_specs=[anyspec] * 4,
        out_specs=[anyspec] * 3,
        scratch_shapes=[
            V((16, ROWS, WIDE), BF),
            V((WIDE, WIDE), BF),
            V((WIDE, WIDE), BF),
            V((16, ROWS, WIDE), BF),
            V((16, 2, HALF, WIDE), BF),
            V((16, 2, HALF, WIDE), BF),
            V((16, 2, PIECE, WIDE), BF),
            V((CH, BAND, WIDE), BF),
            V((16, PIECE, WIDE), BF),
            V((16, PIECE, WIDE), BF),
            V((CH, PIECE, WIDE), F32),
            V((16, ROWS, WIDE), BF),
            V((CH, ROWS, FEAT), F32),
            V((CH, ROWS, FEAT), BF),
            V((CH, ROWS, FEAT), BF),
            V((CH, ROWS, FEAT), BF),
            V((2, 7, TOK, FEAT), BF),
            V((2, TOK, FEAT), BF),
            V((TOK, FEAT), BF),
            V((2, WIDE, WIDE), F32),
            V((2, WIDE, WIDE), BF),
            D((4,)),
            D((2,)),
            D((2,)),
            D((16,)),
            D((16,)),
            D((16,)),
            D((16,)),
            D((16,)),
            D((16,)),
            D((16,)),
            D((16,)),
            D((16,)),
            D((16,)),
            D((16,)),
            D((CH,)),
            D((CH,)),
            D,
            D((CH,)),
            D((2,)),
            D((2,)),
            D((2,)),
            D((3,)),
        ],
        compiler_params=pltpu.CompilerParams(
            collective_id=0, has_side_effects=True, vmem_limit_bytes=58 * 1024 * 1024
        ),
        cost_estimate=pl.CostEstimate(
            flops=12 * 10**9, bytes_accessed=5 * 10**6, transcendentals=10**6
        ),
    )(latents, w_in, w_out, cotangent)


def solution(mesh):
    placed = (P("col", "row"), P("row", "col"), P("col", "row"), P("col", "row"))
    return jax.shard_map(
        per_device,
        mesh=mesh,
        in_specs=placed,
        out_specs=(P("col", "row"), P("row", "col"), P("col", "row")),
        check_vma=False,
    )
```

```python
import jax
import jax.numpy as jnp
from jax import lax
from jax.experimental import pallas as pl
from jax.experimental.pallas import tpu as pltpu
from jax.sharding import PartitionSpec as P

MESH = pl.DeviceIdType.MESH
BF = jnp.bfloat16
F32 = jnp.float32

TOK, FEAT, HID = 128, 384, 1536
ROWS, WIDE = 256, 768
CH = 8
RF0, RF, RB0, RB = 0, 1, 11, 1
GF0, GF, GB0, GB1 = 8, 1, 23, 1
FX, FY = (2, 4, 6, 2), (2, 4, 6, 2)
BX, BY = (3, 6, 9, 3), (3, 6, 9, 3)
UF, UB = 4, 6
COT = 6, 8
TICKS = GB0 + 7 * GB1 + UB + 1
BAND, PART, BIT = 128, 32, 16
PIECE, HALF = 64, 32

NN = (((1,), (0,)), ((), ()))
NT = (((1,), (1,)), ((), ()))
TN = (((0,), (0,)), ((), ()))


def dot(a, b, dims):
    return lax.dot_general(a, b, dims, preferred_element_type=F32)


def kernel(
    lat, w_in, w_out, cot,
    mixed, g_in, g_out,
    X, WI, WO, PT, FAR, CMB, RX, YB, YS, YR, SL, A, MO, MS, MR, MT, MIX, SIDE, OUT, GW, GB,
    s_loc, s_w, s_ws, s_x, s_xs, s_c, s_cs, s_far, s_rx, s_yr, s_ya, s_ag, s_fw,
    s_snd, s_mr, s_ms, s_mix, s_mixs, s_side, s_g, s_gs, s_gl,
):
    row, col = lax.axis_index("row"), lax.axis_index("col")
    x, yh, core = row // 4, (row // 2) % 2, row % 2
    yl, z = col // 8, col % 8

    def dev(x=x, yh=yh, core=core, yl=yl, z=z):
        return ((x * 2 + yh) * 2 + core, yl * 8 + z)

    right, left, across = (x + 1) % 4, (x + 3) % 4, (x + 2) % 4
    east, west = dev(x=right), dev(x=left)
    twin = dev(core=1 - core)
    pair = dev(yh=1 - yh)
    beside = dev(yl=1 - yl)
    up, down = dev(z=(z + 1) % 8), dev(z=(z + 7) % 8)

    barrier = pltpu.get_barrier_semaphore()
    peers = [east, west, twin, pair, beside] + [dev(z=(z + i) % 8) for i in range(1, 8)]
    for peer in peers:
        pl.semaphore_signal(barrier, inc=1, device_id=peer, device_id_type=MESH)

    def send(src, dst, send_sem, recv_sem, to):
        pltpu.make_async_remote_copy(
            src_ref=src, dst_ref=dst, send_sem=send_sem, recv_sem=recv_sem,
            device_id=to, device_id_type=MESH,
        ).start()

    def wait(ref, sem):
        pltpu.make_async_copy(ref, ref, sem).wait()

    def ds(start, size):
        return pl.ds(pl.multiple_of(start, size), size)

    mine = ds(core * WIDE, WIDE)
    other = ds((1 - core) * WIDE, WIDE)
    own, far = pl.ds(0, FEAT), pl.ds(FEAT, FEAT)
    s0, s1 = pl.ds(0, TOK), pl.ds(TOK, TOK)

    local = [
        pltpu.make_async_copy(lat, X.at[0, s0, own], s_loc.at[0]),
        pltpu.make_async_copy(w_in.at[:, mine], WI.at[own], s_loc.at[1]),
        pltpu.make_async_copy(w_out.at[mine], WO.at[:, own], s_loc.at[2]),
        pltpu.make_async_copy(cot, X.at[8, s0, own], s_loc.at[3]),
    ]
    for c in local:
        c.start()

    GW[...] = jnp.zeros_like(GW)
    pl.semaphore_wait(barrier, len(peers))

    def pieces(fwd):
        size = TOK // 2 if fwd else TOK
        return [(q, q * size, size) for q in range(TOK // size)]

    def first(src, j, fwd):
        for q, at, size in pieces(fwd):
            rows, low, high = src.at[pl.ds(at, size)], pl.ds(at, size), pl.ds(TOK + at, size)
            send(rows, X.at[j, high, own], s_xs.at[j], s_x.at[j, q], beside)
            send(rows, X.at[j + 1, low, own], s_xs.at[j], s_x.at[j + 1, q], up)
            send(rows, X.at[j + 1, high, own], s_xs.at[j], s_x.at[j + 1, q], down)
        send(src, X.at[j, s0, far], s_cs.at[j], s_c.at[j], twin)

    def second(j, fwd):
        for q, at, size in pieces(fwd):
            low, high = pl.ds(at, size), pl.ds(TOK + at, size)
            block = X.at[j, high, own]
            wait(block, s_x.at[j, q])
            send(block, X.at[j + 2, low, own], s_xs.at[j], s_x.at[j + 2, q], up)
            send(block, X.at[j + 2, high, own], s_xs.at[j], s_x.at[j + 2, q], down)
        send(X.at[j, s1, own], X.at[j, s1, far], s_cs.at[j], s_c.at[j], twin)

    first(lat, 0, True)
    send(w_in.at[:, other], WI.at[far], s_ws.at[0], s_w.at[0], twin)
    send(w_out.at[other], WO.at[:, far], s_ws.at[1], s_w.at[1], twin)
    second(0, True)
    for c in local:
        c.wait()
    wait(WI.at[own], s_w.at[0])
    wait(WO.at[:, own], s_w.at[1])

    def gather(j, fwd):
        k = j % CH
        for q, at, size in pieces(fwd):
            wait(X.at[j, pl.ds(0, 2 * size), own], s_x.at[j, q])
            s_low, s_high = pl.ds(at, size), pl.ds(TOK + at, size)
            low, high = X.at[j, s_low, own], X.at[j, s_high, own]

            @pl.when(k <= 5)
            def _():
                send(low, X.at[j + 2, s_low, own], s_xs.at[j], s_x.at[j + 2, q], up)

            @pl.when(k <= 4)
            def _():
                send(high, X.at[j + 2, s_high, own], s_xs.at[j], s_x.at[j + 2, q], down)

            @pl.when(k == 6)
            def _():
                send(high, X.at[j + 1, s_high, own], s_xs.at[j], s_x.at[j + 1, q], down)

        whole = X.at[j, :, own]
        send(whole, X.at[j, :, far], s_cs.at[j], s_c.at[j], twin)

    def x_first(j):
        return (j % 2 == 0) | (j % CH == CH - 1)

    def y_first(j):
        return (j % 2 == 1) & (j % CH != CH - 1)

    def when_x(f):
        return lambda j, fwd: pl.when(x_first(j))(lambda: f(j, fwd))

    def when_y(f):
        return lambda j, fwd: pl.when(y_first(j))(lambda: f(j, fwd))

    def pointwise(j, fwd, h, here, rows):
        if fwd:
            cdf = 0.5 * (1.0 + lax.erf(h * 0.7071067811865476))
            pdf = jnp.exp(-0.5 * h * h) * 0.3989422804014327
            A[j, here, :] = (h * cdf).astype(BF)
            SL[j, pl.ds(0, rows), :] = cdf + h * pdf
        else:
            A[j, here, :] = (h * SL[j - CH, pl.ds(0, rows), :]).astype(BF)

    def part(j, fwd):
        wait(X.at[j, :, own], s_c.at[j])

        PT[j] = (dot(X[j], WI[...], NN) if fwd else dot(X[j], WO[...], NT)).astype(BF)
        ss = s_snd.at[j]

        @pl.when(x_first(j))
        def _():
            send(PT.at[j, ds(across * PIECE, HALF)], FAR.at[j, 0], ss, s_far.at[j], east)
            send(PT.at[j, ds(across * PIECE + HALF, HALF)], FAR.at[j, 1], ss, s_far.at[j], west)
            send(PT.at[j, ds(right * PIECE + HALF, HALF)], RX.at[j, 0, pl.ds(HALF, HALF)], ss, s_rx.at[j], east)
            send(PT.at[j, ds(left * PIECE, HALF)], RX.at[j, 1, pl.ds(0, HALF)], ss, s_rx.at[j], west)

        @pl.when(y_first(j))
        def _():
            send(PT.at[j, ds((1 - yh) * BAND, BAND)], YB.at[j // 2], ss, s_yr.at[j], pair)

    def combine(j, fwd):
        wait(FAR.at[j], s_far.at[j])
        ss = s_snd.at[j]
        a = PT[j, ds(right * PIECE, HALF), :].astype(F32) + FAR[j, 0].astype(F32)
        CMB[j, 0] = a.astype(BF)
        b = PT[j, ds(left * PIECE + HALF, HALF), :].astype(F32) + FAR[j, 1].astype(F32)
        CMB[j, 1] = b.astype(BF)
        send(CMB.at[j, 0], RX.at[j, 0, pl.ds(0, HALF)], ss, s_rx.at[j], east)
        send(CMB.at[j, 1], RX.at[j, 1, pl.ds(HALF, HALF)], ss, s_rx.at[j], west)

    def total(j, fwd):
        wait(RX.at[j], s_rx.at[j])
        t = PT[j, ds(x * PIECE, PIECE), :].astype(F32)
        YS[j] = (t + RX[j, 0].astype(F32) + RX[j, 1].astype(F32)).astype(BF)
        send(YS.at[j], YR.at[j], s_snd.at[j], s_yr.at[j], pair)

    def spread(j, fwd):
        wait(YR.at[j], s_yr.at[j])
        here = ds(x * PIECE, PIECE)
        pointwise(j, fwd, YS[j].astype(F32) + YR[j].astype(F32), here, PIECE)
        block = A.at[j, here]
        send(block, block, s_snd.at[j], s_ag.at[j], east)
        send(block, block, s_snd.at[j], s_ag.at[j], west)

    def onward(j, fwd):
        wait(RX.at[j], s_ag.at[j])
        a = A.at[j, ds(left * PIECE, HALF)]
        b = A.at[j, ds(right * PIECE + HALF, HALF)]
        send(a, a, s_snd.at[j], s_fw.at[j], east)
        send(b, b, s_snd.at[j], s_fw.at[j], west)

    band = yh * BAND

    def fold(j, fwd):
        wait(YB.at[j // 2], s_yr.at[j])
        rows = ds(band, BAND)
        PT[j, rows, :] = (PT[j, rows, :].astype(F32) + YB[j // 2].astype(F32)).astype(BF)
        ss = s_snd.at[j]
        lo, hi = pl.ds(0, BIT), pl.ds(BIT, BIT)
        send(PT.at[j, ds(band + across * PART, BIT)], FAR.at[j, 0, lo], ss, s_far.at[j], east)
        send(PT.at[j, ds(band + across * PART + BIT, BIT)], FAR.at[j, 1, lo], ss, s_far.at[j], west)
        send(PT.at[j, ds(band + right * PART + BIT, BIT)], RX.at[j, 0, hi], ss, s_rx.at[j], east)
        send(PT.at[j, ds(band + left * PART, BIT)], RX.at[j, 1, lo], ss, s_rx.at[j], west)

    def combine_y(j, fwd):
        wait(FAR.at[j, 0], s_far.at[j])
        ss = s_snd.at[j]
        lo, hi = pl.ds(0, BIT), pl.ds(BIT, BIT)
        a = PT[j, ds(band + right * PART, BIT), :].astype(F32) + FAR[j, 0, lo, :].astype(F32)
        CMB[j, 0, lo, :] = a.astype(BF)
        b = PT[j, ds(band + left * PART + BIT, BIT), :].astype(F32) + FAR[j, 1, lo, :].astype(F32)
        CMB[j, 1, lo, :] = b.astype(BF)
        send(CMB.at[j, 0, lo], RX.at[j, 0, lo], ss, s_rx.at[j], east)
        send(CMB.at[j, 1, lo], RX.at[j, 1, hi], ss, s_rx.at[j], west)

    def point_y(j, fwd):
        wait(RX.at[j, 0], s_rx.at[j])
        here = ds(band + x * PART, PART)
        h = PT[j, here, :].astype(F32) + RX[j, 0, pl.ds(0, PART), :].astype(F32)
        pointwise(j, fwd, h + RX[j, 1, pl.ds(0, PART), :].astype(F32), here, PART)
        block = A.at[j, here]
        send(block, block, s_snd.at[j], s_ag.at[j], east)
        send(block, block, s_snd.at[j], s_ag.at[j], west)

    def onward_y(j, fwd):
        wait(RX.at[j, 0], s_ag.at[j])
        a = A.at[j, ds(band + left * PART, BIT)]
        b = A.at[j, ds(band + right * PART + BIT, BIT)]
        send(a, a, s_snd.at[j], s_fw.at[j], east)
        send(b, b, s_snd.at[j], s_fw.at[j], west)

    def spread_y(j, fwd):
        wait(YR.at[j, pl.ds(0, PART)], s_fw.at[j])
        block = A.at[j, ds(band, BAND)]
        send(block, block, s_snd.at[j], s_ya.at[j], pair)

    def use(j, fwd):
        pl.when(x_first(j))(lambda: wait(FAR.at[j], s_fw.at[j]))
        pl.when(y_first(j))(lambda: wait(RX.at[j], s_ya.at[j]))
        if not fwd:
            @pl.when(j < 15)
            def _():
                GW[1] = GW[1] + dot(X[j - CH], A[j], TN)

            return

        m = dot(A[j], WO[...], NN)
        MS[j] = m[:, FEAT:].astype(BF)
        send(MS.at[j], MR.at[j], s_ms.at[j], s_mr.at[j], twin)
        MO[j] = m[:, :FEAT]
        GW[0] = GW[0] + dot(A[j], X[j + CH], TN)

        @pl.when(j == CH - 1)
        def _():
            GB[0] = GW[0].astype(BF)
            pltpu.make_async_copy(GB.at[0, :, own], g_out.at[mine], s_gl.at[0]).start()
            send(GB.at[0, :, far], g_out.at[mine], s_gs.at[0], s_g.at[0], twin)

    def mix(j, fwd):
        wait(MS.at[j], s_mr.at[j])
        MT[j] = (MO[j] + MR[j].astype(F32)).astype(BF)
        m = (j + 1) // 2
        below, above = (z + 8 - m) % 8, (z + m) % 8
        low, high = MT.at[j, s0], MT.at[j, s1]
        sems = s_mixs.at[j], s_mix

        @pl.when((j > 0) & (j < CH - 1))
        def _():
            line = (j + 1) % 2
            send(low, MIX.at[line, j - line - 1], *sems, dev(z=below))
            send(high, MIX.at[line, j - line], *sems, dev(z=above))

        @pl.when(j == CH - 1)
        def _():
            send(low, MIX.at[0, 6], *sems, dev(z=above))
            send(high, MIX.at[1, 6], *sems, dev(z=above))

    def stage(f, t, fwd, start, step):
        t = t - start
        due = (t >= 0) & (t < 8 * step) & (t % step == 0)
        pl.when(due)(lambda: f(t // step + (0 if fwd else CH), fwd))

    def reduce_stage(f, t, lags=(0, 0)):
        stage(f, t - lags[0], True, RF0, RF)
        stage(f, t - lags[1], False, RB0, RB)

    def spread_stage(f, t, lags=(0, 0)):
        stage(f, t - lags[0], True, GF0, GF)
        stage(f, t - lags[1], False, GB0, GB1)

    def drain(j, fwd):
        k = j % CH
        wait(A.at[pl.ds(0, 7), pl.ds(0, PIECE)], s_snd.at[j])
        wait(X.at[j, :, own], s_cs.at[j])

        @pl.when(k == 0)
        def _():
            wait(MIX.at[0, pl.ds(0, 5)], s_xs.at[j])

        @pl.when((k > 0) & (k <= 4))
        def _():
            wait(X.at[j, :, own], s_xs.at[j])

        @pl.when((k == 5) | (k == 6))
        def _():
            wait(X.at[j, s0, own], s_xs.at[j])

        if not fwd:
            wait(MS.at[k], s_ms.at[k])

            @pl.when(k > 0)
            def _():
                wait(MT.at[k], s_mixs.at[k])

    def next_gather(j, fwd):
        pl.when(j % CH != CH - 1)(lambda: gather(j + 1, fwd))

    def line_total(line):
        t = MT[0, pl.ds(line * TOK, TOK), :].astype(F32)
        for k in range(7):
            t = t + MIX[line, k].astype(F32)
        return t

    def finish_other():
        wait(MIX, s_mix)
        SIDE[0] = line_total(1).astype(BF)
        send(SIDE.at[0], SIDE.at[1], s_side.at[0], s_side.at[1], beside)

    def finish_own():
        t = line_total(0)
        wait(SIDE.at[1], s_side.at[1])
        OUT[...] = (t + SIDE[1].astype(F32)).astype(BF)
        pltpu.make_async_copy(OUT, mixed, s_gl.at[2]).start()

    def step(t, carry):
        reduce_stage(part, t)
        reduce_stage(next_gather, t)
        spread_stage(when_x(onward), t, (FX[3], BX[3]))
        spread_stage(when_y(spread_y), t, (FY[3], BY[3]))
        spread_stage(when_x(spread), t)
        spread_stage(when_y(onward_y), t)
        reduce_stage(when_y(point_y), t, (FY[2], BY[2]))
        reduce_stage(when_x(total), t, (FX[1], BX[1]))
        reduce_stage(when_y(combine_y), t, (FY[1], BY[1]))
        reduce_stage(when_x(combine), t, (FX[0], BX[0]))
        reduce_stage(when_y(fold), t, (FY[0], BY[0]))
        stage(mix, t - UF - 1, True, GF0, GF)
        spread_stage(use, t, (UF, UB))
        spread_stage(drain, t, (UF, UB))

        pl.when(t == TICKS - 3)(finish_other)

        @pl.when(t == COT[0])
        def _():
            first(cot, CH, False)

        @pl.when(t == COT[1])
        def _():
            second(CH, False)

        return carry

    lax.fori_loop(0, TICKS, step, 0)

    GB[1, far, :] = (GW[1, far, :] + dot(X[CH - 1, :, far], A[15], TN)).astype(BF)
    send(GB.at[1, far], g_in.at[:, mine], s_gs.at[1], s_g.at[1], twin)
    GB[1, own, :] = (GW[1, own, :] + dot(X[CH - 1, :, own], A[15], TN)).astype(BF)
    last = pltpu.make_async_copy(GB.at[1, own], g_in.at[:, mine], s_gl.at[1])
    last.start()

    finish_own()

    wait(WI.at[own], s_ws.at[0])
    wait(WO.at[:, own], s_ws.at[1])

    for i, (ref, half) in enumerate(((g_out.at[mine], GB.at[0, :, own]), (g_in.at[:, mine], GB.at[1, own]))):
        wait(half, s_gs.at[i])
        wait(half, s_g.at[i])
        wait(half, s_gl.at[i])
    wait(SIDE.at[0], s_side.at[0])
    wait(OUT, s_gl.at[2])


def per_device(latents, w_in, w_out, cotangent):
    anyspec = pl.BlockSpec(memory_space=pl.ANY)
    V, D = pltpu.VMEM, pltpu.SemaphoreType.DMA
    return pl.pallas_call(
        kernel,
        out_shape=(V((TOK, FEAT), BF), V((FEAT, HID), BF), V((HID, FEAT), BF)),
        in_specs=[anyspec] * 4,
        out_specs=[anyspec] * 3,
        scratch_shapes=[
            V((16, ROWS, WIDE), BF),
            V((WIDE, WIDE), BF),
            V((WIDE, WIDE), BF),
            V((16, ROWS, WIDE), BF),
            V((16, 2, HALF, WIDE), BF),
            V((16, 2, HALF, WIDE), BF),
            V((16, 2, PIECE, WIDE), BF),
            V((CH, BAND, WIDE), BF),
            V((16, PIECE, WIDE), BF),
            V((16, PIECE, WIDE), BF),
            V((CH, PIECE, WIDE), F32),
            V((16, ROWS, WIDE), BF),
            V((CH, ROWS, FEAT), F32),
            V((CH, ROWS, FEAT), BF),
            V((CH, ROWS, FEAT), BF),
            V((CH, ROWS, FEAT), BF),
            V((2, 7, TOK, FEAT), BF),
            V((2, TOK, FEAT), BF),
            V((TOK, FEAT), BF),
            V((2, WIDE, WIDE), F32),
            V((2, WIDE, WIDE), BF),
            D((4,)),
            D((2,)),
            D((2,)),
            D((16, 2)),
            D((16,)),
            D((16,)),
            D((16,)),
            D((16,)),
            D((16,)),
            D((16,)),
            D((16,)),
            D((16,)),
            D((16,)),
            D((16,)),
            D((CH,)),
            D((CH,)),
            D,
            D((CH,)),
            D((2,)),
            D((2,)),
            D((2,)),
            D((3,)),
        ],
        compiler_params=pltpu.CompilerParams(
            collective_id=0, has_side_effects=True, vmem_limit_bytes=58 * 1024 * 1024
        ),
        cost_estimate=pl.CostEstimate(
            flops=12 * 10**9, bytes_accessed=5 * 10**6, transcendentals=10**6
        ),
    )(latents, w_in, w_out, cotangent)


def solution(mesh):
    placed = (P("col", "row"), P("row", "col"), P("col", "row"), P("col", "row"))
    return jax.shard_map(
        per_device,
        mesh=mesh,
        in_specs=placed,
        out_specs=(P("col", "row"), P("row", "col"), P("col", "row")),
        check_vma=False,
    )
```

```python
import jax
import jax.numpy as jnp
from jax import lax
from jax.experimental import pallas as pl
from jax.experimental.pallas import tpu as pltpu
from jax.sharding import PartitionSpec as P

MESH = pl.DeviceIdType.MESH
BF = jnp.bfloat16
F32 = jnp.float32

TOK, FEAT, HID = 128, 384, 1536
ROWS, WIDE = 256, 768
CH = 8
RF0, RF, RB0, RB = 0, 1, 10, 1
GF0, GF, GB0, GB1 = 9, 1, 22, 1
FX, FY = (2, 4, 6, 2), (2, 4, 6, 2)
BX, BY = (3, 6, 9, 4), (3, 6, 9, 3)
UF, UB = 4, 7
COT = 6, 8
TICKS = GB0 + 7 * GB1 + UB + 1
BAND, PART, BIT = 128, 32, 16
PIECE, HALF = 64, 32

NN = (((1,), (0,)), ((), ()))
NT = (((1,), (1,)), ((), ()))
TN = (((0,), (0,)), ((), ()))


def dot(a, b, dims):
    return lax.dot_general(a, b, dims, preferred_element_type=F32)


def kernel(
    lat, w_in, w_out, cot,
    mixed, g_in, g_out,
    X, WI, WO, PT, FAR, CMB, RX, YB, YS, YR, SL, A, MO, MS, MR, MT, MIX, SIDE, OUT, GW, GB,
    s_loc, s_w, s_ws, s_x, s_xs, s_c, s_cs, s_far, s_rx, s_yr, s_ya, s_ag, s_fw,
    s_snd, s_mr, s_ms, s_mix, s_mixs, s_side, s_g, s_gs, s_gl,
):
    row, col = lax.axis_index("row"), lax.axis_index("col")
    x, yh, core = row // 4, (row // 2) % 2, row % 2
    yl, z = col // 8, col % 8

    def dev(x=x, yh=yh, core=core, yl=yl, z=z):
        return ((x * 2 + yh) * 2 + core, yl * 8 + z)

    right, left, across = (x + 1) % 4, (x + 3) % 4, (x + 2) % 4
    east, west = dev(x=right), dev(x=left)
    twin = dev(core=1 - core)
    pair = dev(yh=1 - yh)
    beside = dev(yl=1 - yl)
    up, down = dev(z=(z + 1) % 8), dev(z=(z + 7) % 8)

    barrier = pltpu.get_barrier_semaphore()
    peers = [east, west, twin, pair, beside] + [dev(z=(z + i) % 8) for i in range(1, 8)]
    for peer in peers:
        pl.semaphore_signal(barrier, inc=1, device_id=peer, device_id_type=MESH)

    def send(src, dst, send_sem, recv_sem, to):
        pltpu.make_async_remote_copy(
            src_ref=src, dst_ref=dst, send_sem=send_sem, recv_sem=recv_sem,
            device_id=to, device_id_type=MESH,
        ).start()

    def wait(ref, sem):
        pltpu.make_async_copy(ref, ref, sem).wait()

    def ds(start, size):
        return pl.ds(pl.multiple_of(start, size), size)

    mine = ds(core * WIDE, WIDE)
    other = ds((1 - core) * WIDE, WIDE)
    own, far = pl.ds(0, FEAT), pl.ds(FEAT, FEAT)
    s0, s1 = pl.ds(0, TOK), pl.ds(TOK, TOK)

    local = [
        pltpu.make_async_copy(lat, X.at[0, s0, own], s_loc.at[0]),
        pltpu.make_async_copy(w_in.at[:, mine], WI.at[own], s_loc.at[1]),
        pltpu.make_async_copy(w_out.at[mine], WO.at[:, own], s_loc.at[2]),
        pltpu.make_async_copy(cot, X.at[8, s0, own], s_loc.at[3]),
    ]
    for c in local:
        c.start()

    GW[...] = jnp.zeros_like(GW)
    pl.semaphore_wait(barrier, len(peers))

    def pieces(fwd):
        size = TOK // 2 if fwd else TOK
        return [(q, q * size, size) for q in range(TOK // size)]

    def first(src, j, fwd):
        for q, at, size in pieces(fwd):
            rows, low, high = src.at[pl.ds(at, size)], pl.ds(at, size), pl.ds(TOK + at, size)
            send(rows, X.at[j, high, own], s_xs.at[j], s_x.at[j, q], beside)
            send(rows, X.at[j + 1, low, own], s_xs.at[j], s_x.at[j + 1, q], up)
            send(rows, X.at[j + 1, high, own], s_xs.at[j], s_x.at[j + 1, q], down)
        send(src, X.at[j, s0, far], s_cs.at[j], s_c.at[j], twin)

    def second(j, fwd):
        for q, at, size in pieces(fwd):
            low, high = pl.ds(at, size), pl.ds(TOK + at, size)
            block = X.at[j, high, own]
            wait(block, s_x.at[j, q])
            send(block, X.at[j + 2, low, own], s_xs.at[j], s_x.at[j + 2, q], up)
            send(block, X.at[j + 2, high, own], s_xs.at[j], s_x.at[j + 2, q], down)
        send(X.at[j, s1, own], X.at[j, s1, far], s_cs.at[j], s_c.at[j], twin)

    first(lat, 0, True)
    send(w_in.at[:, other], WI.at[far], s_ws.at[0], s_w.at[0], twin)
    send(w_out.at[other], WO.at[:, far], s_ws.at[1], s_w.at[1], twin)
    second(0, True)
    for c in local:
        c.wait()
    wait(WI.at[own], s_w.at[0])
    wait(WO.at[:, own], s_w.at[1])

    def gather(j, fwd):
        k = j % CH
        for q, at, size in pieces(fwd):
            wait(X.at[j, pl.ds(0, 2 * size), own], s_x.at[j, q])
            s_low, s_high = pl.ds(at, size), pl.ds(TOK + at, size)
            low, high = X.at[j, s_low, own], X.at[j, s_high, own]

            @pl.when(k <= 5)
            def _():
                send(low, X.at[j + 2, s_low, own], s_xs.at[j], s_x.at[j + 2, q], up)

            @pl.when(k <= 4)
            def _():
                send(high, X.at[j + 2, s_high, own], s_xs.at[j], s_x.at[j + 2, q], down)

            @pl.when(k == 6)
            def _():
                send(high, X.at[j + 1, s_high, own], s_xs.at[j], s_x.at[j + 1, q], down)

        whole = X.at[j, :, own]
        send(whole, X.at[j, :, far], s_cs.at[j], s_c.at[j], twin)

    def x_first(j):
        return (j % 2 == 0) | (j % CH == CH - 1)

    def y_first(j):
        return (j % 2 == 1) & (j % CH != CH - 1)

    def when_x(f):
        return lambda j, fwd: pl.when(x_first(j))(lambda: f(j, fwd))

    def when_y(f):
        return lambda j, fwd: pl.when(y_first(j))(lambda: f(j, fwd))

    def pointwise(j, fwd, h, here, rows):
        if fwd:
            cdf = 0.5 * (1.0 + lax.erf(h * 0.7071067811865476))
            pdf = jnp.exp(-0.5 * h * h) * 0.3989422804014327
            A[j, here, :] = (h * cdf).astype(BF)
            SL[j, pl.ds(0, rows), :] = cdf + h * pdf
        else:
            A[j, here, :] = (h * SL[j - CH, pl.ds(0, rows), :]).astype(BF)

    def part(j, fwd):
        wait(X.at[j, :, own], s_c.at[j])

        PT[j] = (dot(X[j], WI[...], NN) if fwd else dot(X[j], WO[...], NT)).astype(BF)
        ss = s_snd.at[j]

        @pl.when(x_first(j))
        def _():
            send(PT.at[j, ds(across * PIECE, HALF)], FAR.at[j, 0], ss, s_far.at[j], east)
            send(PT.at[j, ds(across * PIECE + HALF, HALF)], FAR.at[j, 1], ss, s_far.at[j], west)
            send(PT.at[j, ds(right * PIECE + HALF, HALF)], RX.at[j, 0, pl.ds(HALF, HALF)], ss, s_rx.at[j], east)
            send(PT.at[j, ds(left * PIECE, HALF)], RX.at[j, 1, pl.ds(0, HALF)], ss, s_rx.at[j], west)

        @pl.when(y_first(j))
        def _():
            send(PT.at[j, ds((1 - yh) * BAND, BAND)], YB.at[j // 2], ss, s_yr.at[j], pair)

    def combine(j, fwd):
        wait(FAR.at[j], s_far.at[j])
        ss = s_snd.at[j]
        a = PT[j, ds(right * PIECE, HALF), :].astype(F32) + FAR[j, 0].astype(F32)
        CMB[j, 0] = a.astype(BF)
        b = PT[j, ds(left * PIECE + HALF, HALF), :].astype(F32) + FAR[j, 1].astype(F32)
        CMB[j, 1] = b.astype(BF)
        send(CMB.at[j, 0], RX.at[j, 0, pl.ds(0, HALF)], ss, s_rx.at[j], east)
        send(CMB.at[j, 1], RX.at[j, 1, pl.ds(HALF, HALF)], ss, s_rx.at[j], west)

    def total(j, fwd):
        wait(RX.at[j], s_rx.at[j])
        t = PT[j, ds(x * PIECE, PIECE), :].astype(F32)
        YS[j] = (t + RX[j, 0].astype(F32) + RX[j, 1].astype(F32)).astype(BF)
        send(YS.at[j], YR.at[j], s_snd.at[j], s_yr.at[j], pair)

    def spread(j, fwd):
        wait(YR.at[j], s_yr.at[j])
        here = ds(x * PIECE, PIECE)
        pointwise(j, fwd, YS[j].astype(F32) + YR[j].astype(F32), here, PIECE)
        block = A.at[j, here]
        send(block, block, s_snd.at[j], s_ag.at[j], east)
        send(block, block, s_snd.at[j], s_ag.at[j], west)

    def onward(j, fwd):
        wait(RX.at[j], s_ag.at[j])
        a = A.at[j, ds(left * PIECE, HALF)]
        b = A.at[j, ds(right * PIECE + HALF, HALF)]
        send(a, a, s_snd.at[j], s_fw.at[j], east)
        send(b, b, s_snd.at[j], s_fw.at[j], west)

    band = yh * BAND

    def fold(j, fwd):
        wait(YB.at[j // 2], s_yr.at[j])
        rows = ds(band, BAND)
        PT[j, rows, :] = (PT[j, rows, :].astype(F32) + YB[j // 2].astype(F32)).astype(BF)
        ss = s_snd.at[j]
        lo, hi = pl.ds(0, BIT), pl.ds(BIT, BIT)
        send(PT.at[j, ds(band + across * PART, BIT)], FAR.at[j, 0, lo], ss, s_far.at[j], east)
        send(PT.at[j, ds(band + across * PART + BIT, BIT)], FAR.at[j, 1, lo], ss, s_far.at[j], west)
        send(PT.at[j, ds(band + right * PART + BIT, BIT)], RX.at[j, 0, hi], ss, s_rx.at[j], east)
        send(PT.at[j, ds(band + left * PART, BIT)], RX.at[j, 1, lo], ss, s_rx.at[j], west)

    def combine_y(j, fwd):
        wait(FAR.at[j, 0], s_far.at[j])
        ss = s_snd.at[j]
        lo, hi = pl.ds(0, BIT), pl.ds(BIT, BIT)
        a = PT[j, ds(band + right * PART, BIT), :].astype(F32) + FAR[j, 0, lo, :].astype(F32)
        CMB[j, 0, lo, :] = a.astype(BF)
        b = PT[j, ds(band + left * PART + BIT, BIT), :].astype(F32) + FAR[j, 1, lo, :].astype(F32)
        CMB[j, 1, lo, :] = b.astype(BF)
        send(CMB.at[j, 0, lo], RX.at[j, 0, lo], ss, s_rx.at[j], east)
        send(CMB.at[j, 1, lo], RX.at[j, 1, hi], ss, s_rx.at[j], west)

    def point_y(j, fwd):
        wait(RX.at[j, 0], s_rx.at[j])
        here = ds(band + x * PART, PART)
        h = PT[j, here, :].astype(F32) + RX[j, 0, pl.ds(0, PART), :].astype(F32)
        pointwise(j, fwd, h + RX[j, 1, pl.ds(0, PART), :].astype(F32), here, PART)
        block = A.at[j, here]
        send(block, block, s_snd.at[j], s_ag.at[j], east)
        send(block, block, s_snd.at[j], s_ag.at[j], west)

    def onward_y(j, fwd):
        wait(RX.at[j, 0], s_ag.at[j])
        a = A.at[j, ds(band + left * PART, BIT)]
        b = A.at[j, ds(band + right * PART + BIT, BIT)]
        send(a, a, s_snd.at[j], s_fw.at[j], east)
        send(b, b, s_snd.at[j], s_fw.at[j], west)

    def spread_y(j, fwd):
        wait(YR.at[j, pl.ds(0, PART)], s_fw.at[j])
        block = A.at[j, ds(band, BAND)]
        send(block, block, s_snd.at[j], s_ya.at[j], pair)

    def use(j, fwd):
        pl.when(x_first(j))(lambda: wait(FAR.at[j], s_fw.at[j]))
        pl.when(y_first(j))(lambda: wait(RX.at[j], s_ya.at[j]))
        if not fwd:
            @pl.when(j < 15)
            def _():
                GW[1] = GW[1] + dot(X[j - CH], A[j], TN)

            return

        m = dot(A[j], WO[...], NN)
        MS[j] = m[:, FEAT:].astype(BF)
        send(MS.at[j], MR.at[j], s_ms.at[j], s_mr.at[j], twin)
        MO[j] = m[:, :FEAT]
        GW[0] = GW[0] + dot(A[j], X[j + CH], TN)

        @pl.when(j == CH - 1)
        def _():
            GB[0] = GW[0].astype(BF)
            pltpu.make_async_copy(GB.at[0, :, own], g_out.at[mine], s_gl.at[0]).start()
            send(GB.at[0, :, far], g_out.at[mine], s_gs.at[0], s_g.at[0], twin)

    def mix(j, fwd):
        wait(MS.at[j], s_mr.at[j])
        MT[j] = (MO[j] + MR[j].astype(F32)).astype(BF)
        m = (j + 1) // 2
        below, above = (z + 8 - m) % 8, (z + m) % 8
        low, high = MT.at[j, s0], MT.at[j, s1]
        sems = s_mixs.at[j], s_mix

        @pl.when((j > 0) & (j < CH - 1))
        def _():
            line = (j + 1) % 2
            send(low, MIX.at[line, j - line - 1], *sems, dev(z=below))
            send(high, MIX.at[line, j - line], *sems, dev(z=above))

        @pl.when(j == CH - 1)
        def _():
            send(low, MIX.at[0, 6], *sems, dev(z=above))
            send(high, MIX.at[1, 6], *sems, dev(z=above))

    def stage(f, t, fwd, start, step):
        t = t - start
        due = (t >= 0) & (t < 8 * step) & (t % step == 0)
        pl.when(due)(lambda: f(t // step + (0 if fwd else CH), fwd))

    def reduce_stage(f, t, lags=(0, 0)):
        stage(f, t - lags[0], True, RF0, RF)
        stage(f, t - lags[1], False, RB0, RB)

    def spread_stage(f, t, lags=(0, 0)):
        stage(f, t - lags[0], True, GF0, GF)
        stage(f, t - lags[1], False, GB0, GB1)

    def drain(j, fwd):
        k = j % CH
        wait(A.at[pl.ds(0, 7), pl.ds(0, PIECE)], s_snd.at[j])
        wait(X.at[j, :, own], s_cs.at[j])

        @pl.when(k == 0)
        def _():
            wait(MIX.at[0, pl.ds(0, 5)], s_xs.at[j])

        @pl.when((k > 0) & (k <= 4))
        def _():
            wait(X.at[j, :, own], s_xs.at[j])

        @pl.when((k == 5) | (k == 6))
        def _():
            wait(X.at[j, s0, own], s_xs.at[j])

        if not fwd:
            wait(MS.at[k], s_ms.at[k])

            @pl.when(k > 0)
            def _():
                wait(MT.at[k], s_mixs.at[k])

    def next_gather(j, fwd):
        pl.when(j % CH != CH - 1)(lambda: gather(j + 1, fwd))

    def line_total(line):
        t = MT[0, pl.ds(line * TOK, TOK), :].astype(F32)
        for k in range(7):
            t = t + MIX[line, k].astype(F32)
        return t

    def finish_other():
        wait(MIX, s_mix)
        SIDE[0] = line_total(1).astype(BF)
        send(SIDE.at[0], SIDE.at[1], s_side.at[0], s_side.at[1], beside)

    def finish_own():
        t = line_total(0)
        wait(SIDE.at[1], s_side.at[1])
        OUT[...] = (t + SIDE[1].astype(F32)).astype(BF)
        pltpu.make_async_copy(OUT, mixed, s_gl.at[2]).start()

    def step(t, carry):
        reduce_stage(part, t)
        reduce_stage(next_gather, t)
        spread_stage(when_x(onward), t, (FX[3], BX[3]))
        spread_stage(when_y(spread_y), t, (FY[3], BY[3]))
        spread_stage(when_x(spread), t)
        spread_stage(when_y(onward_y), t)
        reduce_stage(when_y(point_y), t, (FY[2], BY[2]))
        reduce_stage(when_x(total), t, (FX[1], BX[1]))
        reduce_stage(when_y(combine_y), t, (FY[1], BY[1]))
        reduce_stage(when_x(combine), t, (FX[0], BX[0]))
        reduce_stage(when_y(fold), t, (FY[0], BY[0]))
        stage(mix, t - UF - 1, True, GF0, GF)
        spread_stage(use, t, (UF, UB))
        spread_stage(drain, t, (UF, UB))

        pl.when(t == TICKS - 3)(finish_other)

        @pl.when(t == COT[0])
        def _():
            first(cot, CH, False)

        @pl.when(t == COT[1])
        def _():
            second(CH, False)

        return carry

    lax.fori_loop(0, TICKS, step, 0)

    GB[1, far, :] = (GW[1, far, :] + dot(X[CH - 1, :, far], A[15], TN)).astype(BF)
    send(GB.at[1, far], g_in.at[:, mine], s_gs.at[1], s_g.at[1], twin)
    GB[1, own, :] = (GW[1, own, :] + dot(X[CH - 1, :, own], A[15], TN)).astype(BF)
    last = pltpu.make_async_copy(GB.at[1, own], g_in.at[:, mine], s_gl.at[1])
    last.start()

    finish_own()

    wait(WI.at[own], s_ws.at[0])
    wait(WO.at[:, own], s_ws.at[1])

    for i, (ref, half) in enumerate(((g_out.at[mine], GB.at[0, :, own]), (g_in.at[:, mine], GB.at[1, own]))):
        wait(half, s_gs.at[i])
        wait(half, s_g.at[i])
        wait(half, s_gl.at[i])
    wait(SIDE.at[0], s_side.at[0])
    wait(OUT, s_gl.at[2])


def per_device(latents, w_in, w_out, cotangent):
    anyspec = pl.BlockSpec(memory_space=pl.ANY)
    V, D = pltpu.VMEM, pltpu.SemaphoreType.DMA
    return pl.pallas_call(
        kernel,
        out_shape=(V((TOK, FEAT), BF), V((FEAT, HID), BF), V((HID, FEAT), BF)),
        in_specs=[anyspec] * 4,
        out_specs=[anyspec] * 3,
        scratch_shapes=[
            V((16, ROWS, WIDE), BF),
            V((WIDE, WIDE), BF),
            V((WIDE, WIDE), BF),
            V((16, ROWS, WIDE), BF),
            V((16, 2, HALF, WIDE), BF),
            V((16, 2, HALF, WIDE), BF),
            V((16, 2, PIECE, WIDE), BF),
            V((CH, BAND, WIDE), BF),
            V((16, PIECE, WIDE), BF),
            V((16, PIECE, WIDE), BF),
            V((CH, PIECE, WIDE), F32),
            V((16, ROWS, WIDE), BF),
            V((CH, ROWS, FEAT), F32),
            V((CH, ROWS, FEAT), BF),
            V((CH, ROWS, FEAT), BF),
            V((CH, ROWS, FEAT), BF),
            V((2, 7, TOK, FEAT), BF),
            V((2, TOK, FEAT), BF),
            V((TOK, FEAT), BF),
            V((2, WIDE, WIDE), F32),
            V((2, WIDE, WIDE), BF),
            D((4,)),
            D((2,)),
            D((2,)),
            D((16, 2)),
            D((16,)),
            D((16,)),
            D((16,)),
            D((16,)),
            D((16,)),
            D((16,)),
            D((16,)),
            D((16,)),
            D((16,)),
            D((16,)),
            D((CH,)),
            D((CH,)),
            D,
            D((CH,)),
            D((2,)),
            D((2,)),
            D((2,)),
            D((3,)),
        ],
        compiler_params=pltpu.CompilerParams(
            collective_id=0, has_side_effects=True, vmem_limit_bytes=58 * 1024 * 1024
        ),
        cost_estimate=pl.CostEstimate(
            flops=12 * 10**9, bytes_accessed=5 * 10**6, transcendentals=10**6
        ),
    )(latents, w_in, w_out, cotangent)


def solution(mesh):
    placed = (P("col", "row"), P("row", "col"), P("col", "row"), P("col", "row"))
    return jax.shard_map(
        per_device,
        mesh=mesh,
        in_specs=placed,
        out_specs=(P("col", "row"), P("row", "col"), P("col", "row")),
        check_vma=False,
    )
```

```python
import jax
import jax.numpy as jnp
from jax import lax
from jax.experimental import pallas as pl
from jax.experimental.pallas import tpu as pltpu
from jax.sharding import PartitionSpec as P

MESH = pl.DeviceIdType.MESH
BF = jnp.bfloat16
F32 = jnp.float32

TOK, FEAT, HID = 128, 384, 1536
ROWS, WIDE = 256, 768
CH = 8
RF0, RF, RB0, RB = 0, 1, 10, 1
GF0, GF, GB0, GB1 = 9, 1, 22, 1
FX, FY = (2, 4, 6, 2), (3, 4, 6, 2)
BX, BY = (3, 6, 9, 4), (3, 6, 9, 3)
UF, UB = 4, 7
COT = 6, 8
TICKS = GB0 + 7 * GB1 + UB + 1
BAND, PART, BIT = 128, 32, 16
PIECE, HALF = 64, 32

NN = (((1,), (0,)), ((), ()))
NT = (((1,), (1,)), ((), ()))
TN = (((0,), (0,)), ((), ()))


def dot(a, b, dims):
    return lax.dot_general(a, b, dims, preferred_element_type=F32)


def kernel(
    lat, w_in, w_out, cot,
    mixed, g_in, g_out,
    X, WI, WO, PT, FAR, CMB, RX, YB, YS, YR, SL, A, MO, MS, MR, MT, MIX, SIDE, OUT, GW, GB,
    s_loc, s_w, s_ws, s_x, s_xs, s_c, s_cs, s_far, s_rx, s_yr, s_ya, s_ag, s_fw,
    s_snd, s_mr, s_ms, s_mix, s_mixs, s_side, s_g, s_gs, s_gl,
):
    row, col = lax.axis_index("row"), lax.axis_index("col")
    x, yh, core = row // 4, (row // 2) % 2, row % 2
    yl, z = col // 8, col % 8

    def dev(x=x, yh=yh, core=core, yl=yl, z=z):
        return ((x * 2 + yh) * 2 + core, yl * 8 + z)

    right, left, across = (x + 1) % 4, (x + 3) % 4, (x + 2) % 4
    east, west = dev(x=right), dev(x=left)
    twin = dev(core=1 - core)
    pair = dev(yh=1 - yh)
    beside = dev(yl=1 - yl)
    up, down = dev(z=(z + 1) % 8), dev(z=(z + 7) % 8)

    barrier = pltpu.get_barrier_semaphore()
    peers = [east, west, twin, pair, beside] + [dev(z=(z + i) % 8) for i in range(1, 8)]
    for peer in peers:
        pl.semaphore_signal(barrier, inc=1, device_id=peer, device_id_type=MESH)

    def send(src, dst, send_sem, recv_sem, to):
        pltpu.make_async_remote_copy(
            src_ref=src, dst_ref=dst, send_sem=send_sem, recv_sem=recv_sem,
            device_id=to, device_id_type=MESH,
        ).start()

    def wait(ref, sem):
        pltpu.make_async_copy(ref, ref, sem).wait()

    def ds(start, size):
        return pl.ds(pl.multiple_of(start, size), size)

    mine = ds(core * WIDE, WIDE)
    other = ds((1 - core) * WIDE, WIDE)
    own, far = pl.ds(0, FEAT), pl.ds(FEAT, FEAT)
    s0, s1 = pl.ds(0, TOK), pl.ds(TOK, TOK)

    local = [
        pltpu.make_async_copy(lat, X.at[0, s0, own], s_loc.at[0]),
        pltpu.make_async_copy(w_in.at[:, mine], WI.at[own], s_loc.at[1]),
        pltpu.make_async_copy(w_out.at[mine], WO.at[:, own], s_loc.at[2]),
        pltpu.make_async_copy(cot, X.at[8, s0, own], s_loc.at[3]),
    ]
    for c in local:
        c.start()

    GW[...] = jnp.zeros_like(GW)
    pl.semaphore_wait(barrier, len(peers))

    def pieces(fwd):
        size = TOK // 2 if fwd else TOK
        return [(q, q * size, size) for q in range(TOK // size)]

    def first(src, j, fwd):
        for q, at, size in pieces(fwd):
            rows, low, high = src.at[pl.ds(at, size)], pl.ds(at, size), pl.ds(TOK + at, size)
            send(rows, X.at[j, high, own], s_xs.at[j], s_x.at[j, q], beside)
            send(rows, X.at[j + 1, low, own], s_xs.at[j], s_x.at[j + 1, q], up)
            send(rows, X.at[j + 1, high, own], s_xs.at[j], s_x.at[j + 1, q], down)
        send(src, X.at[j, s0, far], s_cs.at[j], s_c.at[j], twin)

    def second(j, fwd):
        for q, at, size in pieces(fwd):
            low, high = pl.ds(at, size), pl.ds(TOK + at, size)
            block = X.at[j, high, own]
            wait(block, s_x.at[j, q])
            send(block, X.at[j + 2, low, own], s_xs.at[j], s_x.at[j + 2, q], up)
            send(block, X.at[j + 2, high, own], s_xs.at[j], s_x.at[j + 2, q], down)
        send(X.at[j, s1, own], X.at[j, s1, far], s_cs.at[j], s_c.at[j], twin)

    first(lat, 0, True)
    send(w_in.at[:, other], WI.at[far], s_ws.at[0], s_w.at[0], twin)
    send(w_out.at[other], WO.at[:, far], s_ws.at[1], s_w.at[1], twin)
    second(0, True)
    for c in local:
        c.wait()
    wait(WI.at[own], s_w.at[0])
    wait(WO.at[:, own], s_w.at[1])

    def gather(j, fwd):
        k = j % CH
        for q, at, size in pieces(fwd):
            wait(X.at[j, pl.ds(0, 2 * size), own], s_x.at[j, q])
            s_low, s_high = pl.ds(at, size), pl.ds(TOK + at, size)
            low, high = X.at[j, s_low, own], X.at[j, s_high, own]

            @pl.when(k <= 5)
            def _():
                send(low, X.at[j + 2, s_low, own], s_xs.at[j], s_x.at[j + 2, q], up)

            @pl.when(k <= 4)
            def _():
                send(high, X.at[j + 2, s_high, own], s_xs.at[j], s_x.at[j + 2, q], down)

            @pl.when(k == 6)
            def _():
                send(high, X.at[j + 1, s_high, own], s_xs.at[j], s_x.at[j + 1, q], down)

        whole = X.at[j, :, own]
        send(whole, X.at[j, :, far], s_cs.at[j], s_c.at[j], twin)

    def x_first(j):
        return (j % 2 == 0) | (j % CH == CH - 1)

    def y_first(j):
        return (j % 2 == 1) & (j % CH != CH - 1)

    def when_x(f):
        return lambda j, fwd: pl.when(x_first(j))(lambda: f(j, fwd))

    def when_y(f):
        return lambda j, fwd: pl.when(y_first(j))(lambda: f(j, fwd))

    def pointwise(j, fwd, h, here, rows):
        if fwd:
            cdf = 0.5 * (1.0 + lax.erf(h * 0.7071067811865476))
            pdf = jnp.exp(-0.5 * h * h) * 0.3989422804014327
            A[j, here, :] = (h * cdf).astype(BF)
            SL[j, pl.ds(0, rows), :] = cdf + h * pdf
        else:
            A[j, here, :] = (h * SL[j - CH, pl.ds(0, rows), :]).astype(BF)

    def part(j, fwd):
        wait(X.at[j, :, own], s_c.at[j])

        PT[j] = (dot(X[j], WI[...], NN) if fwd else dot(X[j], WO[...], NT)).astype(BF)
        ss = s_snd.at[j]

        @pl.when(x_first(j))
        def _():
            send(PT.at[j, ds(across * PIECE, HALF)], FAR.at[j, 0], ss, s_far.at[j], east)
            send(PT.at[j, ds(across * PIECE + HALF, HALF)], FAR.at[j, 1], ss, s_far.at[j], west)
            send(PT.at[j, ds(right * PIECE + HALF, HALF)], RX.at[j, 0, pl.ds(HALF, HALF)], ss, s_rx.at[j], east)
            send(PT.at[j, ds(left * PIECE, HALF)], RX.at[j, 1, pl.ds(0, HALF)], ss, s_rx.at[j], west)

        @pl.when(y_first(j))
        def _():
            send(PT.at[j, ds((1 - yh) * BAND, BAND)], YB.at[j // 2], ss, s_yr.at[j], pair)

    def combine(j, fwd):
        wait(FAR.at[j], s_far.at[j])
        ss = s_snd.at[j]
        a = PT[j, ds(right * PIECE, HALF), :].astype(F32) + FAR[j, 0].astype(F32)
        CMB[j, 0] = a.astype(BF)
        b = PT[j, ds(left * PIECE + HALF, HALF), :].astype(F32) + FAR[j, 1].astype(F32)
        CMB[j, 1] = b.astype(BF)
        send(CMB.at[j, 0], RX.at[j, 0, pl.ds(0, HALF)], ss, s_rx.at[j], east)
        send(CMB.at[j, 1], RX.at[j, 1, pl.ds(HALF, HALF)], ss, s_rx.at[j], west)

    def total(j, fwd):
        wait(RX.at[j], s_rx.at[j])
        t = PT[j, ds(x * PIECE, PIECE), :].astype(F32)
        YS[j] = (t + RX[j, 0].astype(F32) + RX[j, 1].astype(F32)).astype(BF)
        send(YS.at[j], YR.at[j], s_snd.at[j], s_yr.at[j], pair)

    def spread(j, fwd):
        wait(YR.at[j], s_yr.at[j])
        here = ds(x * PIECE, PIECE)
        pointwise(j, fwd, YS[j].astype(F32) + YR[j].astype(F32), here, PIECE)
        block = A.at[j, here]
        send(block, block, s_snd.at[j], s_ag.at[j], east)
        send(block, block, s_snd.at[j], s_ag.at[j], west)

    def onward(j, fwd):
        wait(RX.at[j], s_ag.at[j])
        a = A.at[j, ds(left * PIECE, HALF)]
        b = A.at[j, ds(right * PIECE + HALF, HALF)]
        send(a, a, s_snd.at[j], s_fw.at[j], east)
        send(b, b, s_snd.at[j], s_fw.at[j], west)

    band = yh * BAND

    def fold(j, fwd):
        wait(YB.at[j // 2], s_yr.at[j])
        rows = ds(band, BAND)
        PT[j, rows, :] = (PT[j, rows, :].astype(F32) + YB[j // 2].astype(F32)).astype(BF)
        ss = s_snd.at[j]
        lo, hi = pl.ds(0, BIT), pl.ds(BIT, BIT)
        send(PT.at[j, ds(band + across * PART, BIT)], FAR.at[j, 0, lo], ss, s_far.at[j], east)
        send(PT.at[j, ds(band + across * PART + BIT, BIT)], FAR.at[j, 1, lo], ss, s_far.at[j], west)
        send(PT.at[j, ds(band + right * PART + BIT, BIT)], RX.at[j, 0, hi], ss, s_rx.at[j], east)
        send(PT.at[j, ds(band + left * PART, BIT)], RX.at[j, 1, lo], ss, s_rx.at[j], west)

    def combine_y(j, fwd):
        wait(FAR.at[j, 0], s_far.at[j])
        ss = s_snd.at[j]
        lo, hi = pl.ds(0, BIT), pl.ds(BIT, BIT)
        a = PT[j, ds(band + right * PART, BIT), :].astype(F32) + FAR[j, 0, lo, :].astype(F32)
        CMB[j, 0, lo, :] = a.astype(BF)
        b = PT[j, ds(band + left * PART + BIT, BIT), :].astype(F32) + FAR[j, 1, lo, :].astype(F32)
        CMB[j, 1, lo, :] = b.astype(BF)
        send(CMB.at[j, 0, lo], RX.at[j, 0, lo], ss, s_rx.at[j], east)
        send(CMB.at[j, 1, lo], RX.at[j, 1, hi], ss, s_rx.at[j], west)

    def point_y(j, fwd):
        wait(RX.at[j, 0], s_rx.at[j])
        here = ds(band + x * PART, PART)
        h = PT[j, here, :].astype(F32) + RX[j, 0, pl.ds(0, PART), :].astype(F32)
        pointwise(j, fwd, h + RX[j, 1, pl.ds(0, PART), :].astype(F32), here, PART)
        block = A.at[j, here]
        send(block, block, s_snd.at[j], s_ag.at[j], east)
        send(block, block, s_snd.at[j], s_ag.at[j], west)

    def onward_y(j, fwd):
        wait(RX.at[j, 0], s_ag.at[j])
        a = A.at[j, ds(band + left * PART, BIT)]
        b = A.at[j, ds(band + right * PART + BIT, BIT)]
        send(a, a, s_snd.at[j], s_fw.at[j], east)
        send(b, b, s_snd.at[j], s_fw.at[j], west)

    def spread_y(j, fwd):
        wait(YR.at[j, pl.ds(0, PART)], s_fw.at[j])
        block = A.at[j, ds(band, BAND)]
        send(block, block, s_snd.at[j], s_ya.at[j], pair)

    def use(j, fwd):
        pl.when(x_first(j))(lambda: wait(FAR.at[j], s_fw.at[j]))
        pl.when(y_first(j))(lambda: wait(RX.at[j], s_ya.at[j]))
        if not fwd:
            @pl.when(j < 15)
            def _():
                GW[1] = GW[1] + dot(X[j - CH], A[j], TN)

            return

        m = dot(A[j], WO[...], NN)
        MS[j] = m[:, FEAT:].astype(BF)
        send(MS.at[j], MR.at[j], s_ms.at[j], s_mr.at[j], twin)
        MO[j] = m[:, :FEAT]
        GW[0] = GW[0] + dot(A[j], X[j + CH], TN)

        @pl.when(j == CH - 1)
        def _():
            GB[0] = GW[0].astype(BF)
            pltpu.make_async_copy(GB.at[0, :, own], g_out.at[mine], s_gl.at[0]).start()
            send(GB.at[0, :, far], g_out.at[mine], s_gs.at[0], s_g.at[0], twin)

    def mix(j, fwd):
        wait(MS.at[j], s_mr.at[j])
        MT[j] = (MO[j] + MR[j].astype(F32)).astype(BF)
        m = (j + 1) // 2
        below, above = (z + 8 - m) % 8, (z + m) % 8
        low, high = MT.at[j, s0], MT.at[j, s1]
        sems = s_mixs.at[j], s_mix

        @pl.when((j > 0) & (j < CH - 1))
        def _():
            line = (j + 1) % 2
            send(low, MIX.at[line, j - line - 1], *sems, dev(z=below))
            send(high, MIX.at[line, j - line], *sems, dev(z=above))

        @pl.when(j == CH - 1)
        def _():
            send(low, MIX.at[0, 6], *sems, dev(z=above))
            send(high, MIX.at[1, 6], *sems, dev(z=above))

    def stage(f, t, fwd, start, step):
        t = t - start
        due = (t >= 0) & (t < 8 * step) & (t % step == 0)
        pl.when(due)(lambda: f(t // step + (0 if fwd else CH), fwd))

    def reduce_stage(f, t, lags=(0, 0)):
        stage(f, t - lags[0], True, RF0, RF)
        stage(f, t - lags[1], False, RB0, RB)

    def spread_stage(f, t, lags=(0, 0)):
        stage(f, t - lags[0], True, GF0, GF)
        stage(f, t - lags[1], False, GB0, GB1)

    def drain(j, fwd):
        k = j % CH
        wait(A.at[pl.ds(0, 7), pl.ds(0, PIECE)], s_snd.at[j])
        wait(X.at[j, :, own], s_cs.at[j])

        @pl.when(k == 0)
        def _():
            wait(MIX.at[0, pl.ds(0, 5)], s_xs.at[j])

        @pl.when((k > 0) & (k <= 4))
        def _():
            wait(X.at[j, :, own], s_xs.at[j])

        @pl.when((k == 5) | (k == 6))
        def _():
            wait(X.at[j, s0, own], s_xs.at[j])

        if not fwd:
            wait(MS.at[k], s_ms.at[k])

            @pl.when(k > 0)
            def _():
                wait(MT.at[k], s_mixs.at[k])

    def next_gather(j, fwd):
        pl.when(j % CH != CH - 1)(lambda: gather(j + 1, fwd))

    def line_total(line):
        t = MT[0, pl.ds(line * TOK, TOK), :].astype(F32)
        for k in range(7):
            t = t + MIX[line, k].astype(F32)
        return t

    def finish_other():
        wait(MIX, s_mix)
        SIDE[0] = line_total(1).astype(BF)
        send(SIDE.at[0], SIDE.at[1], s_side.at[0], s_side.at[1], beside)

    def finish_own():
        t = line_total(0)
        wait(SIDE.at[1], s_side.at[1])
        OUT[...] = (t + SIDE[1].astype(F32)).astype(BF)
        pltpu.make_async_copy(OUT, mixed, s_gl.at[2]).start()

    def step(t, carry):
        reduce_stage(part, t)
        reduce_stage(next_gather, t)
        spread_stage(when_x(onward), t, (FX[3], BX[3]))
        spread_stage(when_y(spread_y), t, (FY[3], BY[3]))
        spread_stage(when_x(spread), t)
        spread_stage(when_y(onward_y), t)
        reduce_stage(when_y(point_y), t, (FY[2], BY[2]))
        reduce_stage(when_x(total), t, (FX[1], BX[1]))
        reduce_stage(when_y(combine_y), t, (FY[1], BY[1]))
        reduce_stage(when_x(combine), t, (FX[0], BX[0]))
        reduce_stage(when_y(fold), t, (FY[0], BY[0]))
        stage(mix, t - UF - 1, True, GF0, GF)
        spread_stage(use, t, (UF, UB))
        spread_stage(drain, t, (UF, UB))

        pl.when(t == TICKS - 3)(finish_other)

        @pl.when(t == COT[0])
        def _():
            first(cot, CH, False)

        @pl.when(t == COT[1])
        def _():
            second(CH, False)

        return carry

    lax.fori_loop(0, TICKS, step, 0)

    GB[1, far, :] = (GW[1, far, :] + dot(X[CH - 1, :, far], A[15], TN)).astype(BF)
    send(GB.at[1, far], g_in.at[:, mine], s_gs.at[1], s_g.at[1], twin)
    GB[1, own, :] = (GW[1, own, :] + dot(X[CH - 1, :, own], A[15], TN)).astype(BF)
    last = pltpu.make_async_copy(GB.at[1, own], g_in.at[:, mine], s_gl.at[1])
    last.start()

    finish_own()

    wait(WI.at[own], s_ws.at[0])
    wait(WO.at[:, own], s_ws.at[1])

    for i, (ref, half) in enumerate(((g_out.at[mine], GB.at[0, :, own]), (g_in.at[:, mine], GB.at[1, own]))):
        wait(half, s_gs.at[i])
        wait(half, s_g.at[i])
        wait(half, s_gl.at[i])
    wait(SIDE.at[0], s_side.at[0])
    wait(OUT, s_gl.at[2])


def per_device(latents, w_in, w_out, cotangent):
    anyspec = pl.BlockSpec(memory_space=pl.ANY)
    V, D = pltpu.VMEM, pltpu.SemaphoreType.DMA
    return pl.pallas_call(
        kernel,
        out_shape=(V((TOK, FEAT), BF), V((FEAT, HID), BF), V((HID, FEAT), BF)),
        in_specs=[anyspec] * 4,
        out_specs=[anyspec] * 3,
        scratch_shapes=[
            V((16, ROWS, WIDE), BF),
            V((WIDE, WIDE), BF),
            V((WIDE, WIDE), BF),
            V((16, ROWS, WIDE), BF),
            V((16, 2, HALF, WIDE), BF),
            V((16, 2, HALF, WIDE), BF),
            V((16, 2, PIECE, WIDE), BF),
            V((CH, BAND, WIDE), BF),
            V((16, PIECE, WIDE), BF),
            V((16, PIECE, WIDE), BF),
            V((CH, PIECE, WIDE), F32),
            V((16, ROWS, WIDE), BF),
            V((CH, ROWS, FEAT), F32),
            V((CH, ROWS, FEAT), BF),
            V((CH, ROWS, FEAT), BF),
            V((CH, ROWS, FEAT), BF),
            V((2, 7, TOK, FEAT), BF),
            V((2, TOK, FEAT), BF),
            V((TOK, FEAT), BF),
            V((2, WIDE, WIDE), F32),
            V((2, WIDE, WIDE), BF),
            D((4,)),
            D((2,)),
            D((2,)),
            D((16, 2)),
            D((16,)),
            D((16,)),
            D((16,)),
            D((16,)),
            D((16,)),
            D((16,)),
            D((16,)),
            D((16,)),
            D((16,)),
            D((16,)),
            D((CH,)),
            D((CH,)),
            D,
            D((CH,)),
            D((2,)),
            D((2,)),
            D((2,)),
            D((3,)),
        ],
        compiler_params=pltpu.CompilerParams(
            collective_id=0, has_side_effects=True, vmem_limit_bytes=58 * 1024 * 1024
        ),
        cost_estimate=pl.CostEstimate(
            flops=12 * 10**9, bytes_accessed=5 * 10**6, transcendentals=10**6
        ),
    )(latents, w_in, w_out, cotangent)


def solution(mesh):
    placed = (P("col", "row"), P("row", "col"), P("col", "row"), P("col", "row"))
    return jax.shard_map(
        per_device,
        mesh=mesh,
        in_specs=placed,
        out_specs=(P("col", "row"), P("row", "col"), P("col", "row")),
        check_vma=False,
    )
```
